32 devices in a mesh: seq: 8 (over z, x), head: 2 (over y), batch: 2 (over core).
Axes of the slice: x: 2, y: 2, z: 4, core: 2. Of those that a mesh axis runs over, the one named last changes fastest.
Arguments:
- query_states: bfloat16 [4096, 1024], P(('batch', 'seq'), 'head'), parts along dimension 0, may hold values from -8 to 8
- key_states: bfloat16 [4096, 1024], P(('batch', 'seq'), 'head'), parts along dimension 0, may hold values from -8 to 8
- value_states: bfloat16 [4096, 1024], P(('batch', 'seq'), 'head'), parts along dimension 0, may hold values from -6 to 6
- out_grad: bfloat16 [4096, 1024], P(('batch', 'seq'), 'head'), parts along dimension 0, may hold values from -192 to 192
- head_offsets: int32 [8], P('head'), may hold values from 0 to 2047
Outputs:
- query_grad: bfloat16 [4096, 1024], P(('batch', 'seq'), 'head'), parts along dimension 0
- key_grad: bfloat16 [4096, 1024], P(('batch', 'seq'), 'head'), parts along dimension 0
- value_grad: bfloat16 [4096, 1024], P(('batch', 'seq'), 'head'), parts along dimension 0
The draws below stay inside these ranges and needn't reach their ends.
There are 2 independent parts, one for each index of `batch`. The reference program is written for one: setup_inputs(seed, part) draws one part's arguments, and reference() takes and returns one part's arrays. A program takes and returns all parts, laid end to end along the dimension named above; an argument that names none is the same for every part. Nothing has to cross between parts.
All inputs are finite; a program needn't handle non-finite values.
Results may differ from the reference program's by a relative error of at most 0.0056.
Values may be sent and summed in bfloat16 or wider, within the bound.
A program may use at most 128 MiB of HBM per device.

```python
import jax
import jax.numpy as jnp
from jax import lax

HD = 128
WINDOW = 1024
S_DEV = 256
HEADS = 8
SEQ = 2048
N_SEQ = 8


def paired_fields(key):
    row_total = SEQ
    col_total = HEADS * HD
    key_query = jax.random.fold_in(key, 101)
    key_keys = jax.random.fold_in(key, 102)
    base_query = jnp.clip(jax.random.normal(key_query, (row_total, col_total), jnp.float32), -4.0, 4.0)
    base_keys = jnp.clip(jax.random.normal(key_keys, (row_total, col_total), jnp.float32), -4.0, 4.0)
    return (base_query.astype(jnp.bfloat16), base_keys.astype(jnp.bfloat16))


def draw_query_states(key, part):
    return paired_fields(key)[0]


def draw_key_states(key, part):
    return paired_fields(key)[1]


def place_ends(array, stream_key, low, top_value):
    extent = array.shape
    spot = [jax.random.randint(jax.random.fold_in(stream_key, axis), (), 0, extent[axis]) for axis in range(len(extent))]
    array = array.at[tuple(spot)].set(low)
    longest = extent.index(max(extent))
    spot[longest] = (spot[longest] + 1) % extent[longest]
    return array.at[tuple(spot)].set(top_value)


def level_of(stream_key, shape, shards, low, top_value):
    def one(axis_at, blocks):
        heights = jax.random.uniform(jax.random.fold_in(jax.random.fold_in(stream_key, 6), axis_at), (blocks,), jnp.float32, low / len(shards), top_value / len(shards))
        return jnp.repeat(jnp.exp(heights), shape[axis_at] // blocks).reshape((-1,) + (1,) * (len(shape) - axis_at - 1))

    gain = one(*shards[0])
    for cut in shards[1:]:
        gain = gain * one(*cut)
    return gain


def normal_values(rng, dims, scale, most, cuts=(), kind=jnp.bfloat16):
    entries = scale * jax.random.normal(rng, dims, jnp.float32)
    if cuts:
        entries = entries * level_of(rng, dims, cuts, -0.22, 0.18)
    return jnp.clip(entries, -most, most).astype(kind)


def setup_inputs(seed: int = 0, part: int = 0) -> dict:
    key_list = jax.random.split(jax.random.key(seed), 6)
    part_splits = jax.random.split(jax.random.fold_in(key_list[5], part), 6)
    return {
        "query_states": draw_query_states(jax.random.fold_in(jax.random.fold_in(key_list[5], part), 71), part),
        "key_states": draw_key_states(jax.random.fold_in(jax.random.fold_in(key_list[5], part), 71), part),
        "value_states": normal_values(part_splits[2], (SEQ, HEADS * HD), 1.0, 6.0, ((0, 8), (1, 2))),
        "out_grad": normal_values(part_splits[3], (SEQ, HEADS * HD), 32.0, 192.0, ((0, 8), (1, 2))),
        "head_offsets": place_ends(jax.random.randint(key_list[4], (HEADS,), 0, SEQ), jax.random.fold_in(key_list[4], 1), 0, SEQ - 1).astype(jnp.int32),
    }


masked_score = -1.0e30


def forward_part(queries, keys_in, values_in, allowed, softmax_scale):
    scores = jnp.dot(queries, keys_in.T, preferred_element_type=jnp.float32) * softmax_scale
    scores = jnp.where(allowed, scores, masked_score)
    row_max = jnp.max(scores, axis=-1)
    weights = jnp.exp(scores - row_max[..., None])
    row_sum = jnp.sum(weights, axis=-1)
    row_out = jnp.dot(weights.astype(jnp.bfloat16), values_in, preferred_element_type=jnp.float32)
    return row_max, row_sum, row_out


def backward_part(queries, keys_in, values_in, grads, allowed, log_norm, grad_dot, softmax_scale):
    scores = jnp.dot(queries, keys_in.T, preferred_element_type=jnp.float32) * softmax_scale
    scores = jnp.where(allowed, scores, masked_score)
    weights = jnp.exp(scores - log_norm[..., None])
    grad_values = jnp.dot(weights.astype(jnp.bfloat16).T, grads, preferred_element_type=jnp.float32)
    grad_probs = jnp.dot(grads, values_in.T, preferred_element_type=jnp.float32)
    grad_scores = (weights * (grad_probs - grad_dot[..., None])).astype(jnp.bfloat16)
    grad_queries = jnp.dot(grad_scores, keys_in, preferred_element_type=jnp.float32) * softmax_scale
    grad_keys = jnp.dot(grad_scores.T, queries, preferred_element_type=jnp.float32) * softmax_scale
    return grad_queries, grad_keys, grad_values


def merge_stats(first_stats, second_stats):
    row_max = jnp.maximum(first_stats[0], second_stats[0])
    first_factor = jnp.exp(first_stats[0] - row_max)
    second_factor = jnp.exp(second_stats[0] - row_max)
    row_sum = first_stats[1] * first_factor + second_stats[1] * second_factor
    row_out = first_stats[2] * first_factor[..., None] + second_stats[2] * second_factor[..., None]
    return row_max, row_sum, row_out


def pick_rows(source, stride, first_row):
    shaped = source.reshape((source.shape[0] // stride, stride) + source.shape[1:])
    return lax.dynamic_slice_in_dim(shaped, first_row, 1, axis=1)[:, 0]


def put_rows(source, stride, first_row, update):
    shaped = source.reshape((source.shape[0] // stride, stride) + source.shape[1:])
    return lax.dynamic_update_slice_in_dim(shaped, update[:, None], first_row, axis=1).reshape(source.shape)


def one_head(inputs):
    query, key_rows, value_rows, grad_rows, head_offset = inputs
    softmax_scale = HD ** -0.5
    reach_slabs = WINDOW // S_DEV
    span_cols = (reach_slabs + 1) * S_DEV
    padding = jnp.zeros((reach_slabs * S_DEV, HD), jnp.bfloat16)
    key_pad = jnp.concatenate([padding, key_rows], axis=0)
    value_pad = jnp.concatenate([padding, value_rows], axis=0)
    local_rows = jnp.arange(S_DEV, dtype=jnp.int32)[:, None]
    key_cols = jnp.arange(span_cols, dtype=jnp.int32)[None, :]
    distance = local_rows - key_cols + reach_slabs * S_DEV

    def near_inputs(slab_index):
        first_row = (slab_index * S_DEV).astype(jnp.int32)
        allowed = (distance >= 0) & (distance < WINDOW) & (first_row + key_cols - reach_slabs * S_DEV >= 0)
        return (lax.dynamic_slice_in_dim(query, first_row, S_DEV),
                lax.dynamic_slice_in_dim(key_pad, first_row, span_cols),
                lax.dynamic_slice_in_dim(value_pad, first_row, span_cols),
                lax.dynamic_slice_in_dim(grad_rows, first_row, S_DEV),
                allowed, first_row)

    def near_forward(slab_index):
        q_part, k_part, v_part, g_part, allowed, first_row = near_inputs(slab_index)
        return forward_part(q_part, k_part, v_part, allowed, softmax_scale)

    slab_list = jnp.arange(N_SEQ, dtype=jnp.int32)
    row_max, row_sum, row_out = lax.map(near_forward, slab_list)
    stats = (row_max.reshape(SEQ), row_sum.reshape(SEQ), row_out.reshape(SEQ, HD))
    level_count = N_SEQ.bit_length() - 1
    causal = jnp.arange(S_DEV, dtype=jnp.int32)[None, :] <= jnp.arange(S_DEV, dtype=jnp.int32)[:, None]
    for level_num in range(1, level_count + 1):
        stride = 2 ** level_num
        first_row = (head_offset % stride).astype(jnp.int32)
        segments = N_SEQ // stride
        sparse_q = pick_rows(query, stride, first_row).reshape(segments, S_DEV, HD)
        sparse_k = pick_rows(key_rows, stride, first_row).reshape(segments, S_DEV, HD)
        sparse_v = pick_rows(value_rows, stride, first_row).reshape(segments, S_DEV, HD)
        update = jax.vmap(forward_part, in_axes=(0, 0, 0, None, None))(sparse_q, sparse_k, sparse_v, causal, softmax_scale)
        update = (update[0].reshape(-1), update[1].reshape(-1), update[2].reshape(-1, HD))
        current = tuple(pick_rows(member, stride, first_row) for member in stats)
        merged = merge_stats(current, update)
        stats = tuple(put_rows(member, stride, first_row, fresh) for member, fresh in zip(stats, merged))
    log_norm = stats[0] + jnp.log(stats[1])
    out_rows = stats[2] / stats[1][:, None]
    grad_dot = jnp.sum(grad_rows.astype(jnp.float32) * out_rows, axis=-1)

    def near_backward(slab_index):
        q_part, k_part, v_part, g_part, allowed, first_row = near_inputs(slab_index)
        return backward_part(q_part, k_part, v_part, g_part, allowed,
                             lax.dynamic_slice_in_dim(log_norm, first_row, S_DEV),
                             lax.dynamic_slice_in_dim(grad_dot, first_row, S_DEV), softmax_scale)

    grad_query, near_key, near_value = lax.map(near_backward, slab_list)
    grad_query = grad_query.reshape(SEQ, HD)
    near_key = near_key.reshape(N_SEQ, reach_slabs + 1, S_DEV, HD)
    near_value = near_value.reshape(N_SEQ, reach_slabs + 1, S_DEV, HD)
    grad_key = jnp.zeros((N_SEQ, S_DEV, HD), jnp.float32)
    grad_value = jnp.zeros((N_SEQ, S_DEV, HD), jnp.float32)
    for block_index in range(reach_slabs + 1):
        behind = reach_slabs - block_index
        if behind < N_SEQ:
            grad_key = grad_key + jnp.pad(near_key[behind:, block_index], ((0, behind), (0, 0), (0, 0)))
            grad_value = grad_value + jnp.pad(near_value[behind:, block_index], ((0, behind), (0, 0), (0, 0)))
    grad_key = grad_key.reshape(SEQ, HD)
    grad_value = grad_value.reshape(SEQ, HD)
    for level_num in range(1, level_count + 1):
        stride = 2 ** level_num
        first_row = (head_offset % stride).astype(jnp.int32)
        segments = N_SEQ // stride
        sparse_q = pick_rows(query, stride, first_row).reshape(segments, S_DEV, HD)
        sparse_k = pick_rows(key_rows, stride, first_row).reshape(segments, S_DEV, HD)
        sparse_v = pick_rows(value_rows, stride, first_row).reshape(segments, S_DEV, HD)
        sparse_g = pick_rows(grad_rows, stride, first_row).reshape(segments, S_DEV, HD)
        sparse_norm = pick_rows(log_norm, stride, first_row).reshape(segments, S_DEV)
        sparse_dot = pick_rows(grad_dot, stride, first_row).reshape(segments, S_DEV)
        level_query, level_key, level_value = jax.vmap(backward_part, in_axes=(0, 0, 0, 0, None, 0, 0, None))(
            sparse_q, sparse_k, sparse_v, sparse_g, causal, sparse_norm, sparse_dot, softmax_scale)
        grad_query = put_rows(grad_query, stride, first_row, pick_rows(grad_query, stride, first_row) + level_query.reshape(-1, HD))
        grad_key = put_rows(grad_key, stride, first_row, pick_rows(grad_key, stride, first_row) + level_key.reshape(-1, HD))
        grad_value = put_rows(grad_value, stride, first_row, pick_rows(grad_value, stride, first_row) + level_value.reshape(-1, HD))
    return grad_query, grad_key, grad_value


def reference(query_states, key_states, value_states, out_grad, head_offsets):
    def split_heads(source):
        return source.reshape(SEQ, HEADS, HD).transpose(1, 0, 2)

    def join_heads(source):
        return source.transpose(1, 0, 2).reshape(SEQ, HEADS * HD).astype(jnp.bfloat16)

    grad_query, grad_key, grad_value = lax.map(one_head, (split_heads(query_states), split_heads(key_states),
                                                         split_heads(value_states), split_heads(out_grad), head_offsets))
    return join_heads(grad_query), join_heads(grad_key), join_heads(grad_value)
```

```python
import functools

import jax
import jax.numpy as jnp
from jax import lax
from jax.experimental import pallas as pl
from jax.experimental.pallas import tpu as pltpu
from jax.sharding import PartitionSpec as P

WINDOW = 1024
MASKED = -1e30


def contract(left, right, left_dim, right_dim):
    return lax.dot_general(
        left, right, (((left_dim,), (right_dim,)), ((), ())), preferred_element_type=jnp.float32
    )


def kernel(
    devices,
    batches,
    heads,
    off_ref,
    key_ref,
    value_ref,
    query_ref,
    grad_ref,
    dq_ref,
    dk_ref,
    dv_ref,
    kv,
    qg,
    scores,
    probs,
    level,
    total,
    dq_out,
    part_out,
    part_in,
    kv_out,
    in_send,
    kv_recv,
    qg_recv,
    peer_send,
    part_send,
    part_recv,
    out_send,
    out_recv,
):
    rows, width = query_ref.shape[0], query_ref.shape[1] // heads
    spots = devices // (heads * batches)
    group = spots * batches
    slots = devices // group
    level_count = devices.bit_length() - 1
    scale = width ** (-0.5)

    seq, batch = lax.axis_index("seq"), lax.axis_index("batch")
    unit = seq // spots
    head, sequence = unit // batches, unit % batches
    share = (seq % spots) * batches + batch
    home_share, home_slot = seq % group, seq // group
    at_home = (sequence == batch) & (home_share == share)

    def worker(h):
        place = {"seq": (h * batches + batch) * spots + home_share // batches}
        place["batch"] = home_share % batches
        return place, at_home & (head == h)

    def owner(t):
        return {"seq": share + group * t, "batch": sequence}, at_home & (home_slot == t)

    def peer(r):
        other = (share + r) % group
        return other, {"seq": unit * spots + other // batches, "batch": other % batches}

    def remote(src, dst, send_sem, recv_sem, place):
        return pltpu.make_async_remote_copy(
            src_ref=src,
            dst_ref=dst,
            send_sem=send_sem,
            recv_sem=recv_sem,
            device_id=place,
            device_id_type=pl.DeviceIdType.MESH,
        )

    def move(src, dst, send_sem, recv_sem, place, same):
        @pl.when(same)
        def _():
            pltpu.make_async_copy(src, dst, recv_sem).start()

        @pl.when(jnp.logical_not(same))
        def _():
            remote(src, dst, send_sem, recv_sem, place).start()

    def sent(src, dst, send_sem, recv_sem, place, same):
        @pl.when(jnp.logical_not(same))
        def _():
            remote(src, dst, send_sem, recv_sem, place).wait_send()

    def landed(ref, sem):
        pltpu.make_async_copy(ref, ref, sem).wait()

    barrier = pltpu.get_barrier_semaphore()

    def greet(place):
        pl.semaphore_signal(barrier, inc=1, device_id=place, device_id_type=pl.DeviceIdType.MESH)

    for place, same in [worker(h) for h in range(heads)] + [owner(t) for t in range(slots)]:
        pl.when(jnp.logical_not(same))(functools.partial(greet, place))
    for r in range(1, group):
        greet(peer(r)[1])
    own = jnp.where(at_home, 1, 0)
    pl.semaphore_wait(barrier, heads + slots - 2 * own + group - 1)

    def inward(a, h):
        source = (key_ref, value_ref, query_ref, grad_ref)[a]
        src = source.at[:, pl.ds(h * width, width)]
        if a < 2:
            dst, recv = kv.at[a, seq], kv_recv.at[a, seq]
        else:
            dst, recv = qg.at[a - 2, home_slot], qg_recv.at[a - 2, home_slot]
        return (src, dst, in_send.at[a, h], recv) + worker(h)

    for a in range(4):
        for h in range(heads):
            move(*inward(a, h))

    offset = off_ref[head]
    key_row = lax.broadcasted_iota(jnp.int32, (rows, rows), 0)
    query_row = lax.broadcasted_iota(jnp.int32, (rows, rows), 1)
    apart = (key_row ^ offset) | (query_row ^ offset)
    matched = jnp.zeros((rows, rows), jnp.float32)
    for l in range(1, level_count + 1):
        matched += jnp.where(apart & (2**l - 1) == 0, 1.0, 0.0)
    level[...] = matched

    def clear(j, _):
        total[0, j] = jnp.zeros((rows, width), jnp.float32)
        total[1, j] = jnp.zeros((rows, width), jnp.float32)
        return 0

    lax.fori_loop(0, devices, clear, 0)

    def shared(a, t, r):
        slab = share + group * t
        block = kv.at[a, slab]
        return remote(block, block, peer_send.at[r - 1, a, t], kv_recv.at[a, slab], peer(r)[1])

    for t in range(slots):
        for a in range(2):
            slab = share + group * t
            landed(kv.at[a, slab], kv_recv.at[a, slab])
            for r in range(1, group):
                shared(a, t, r).start()

    def outward(a, t):
        src = dq_out.at[t] if a == 0 else kv_out.at[a - 1, t]
        dst = (dq_ref, dk_ref, dv_ref)[a].at[:, pl.ds(pl.multiple_of(head * width, width), width)]
        return (src, dst, out_send.at[a, t], out_recv.at[a, head]) + owner(t)

    def work(t):
        slab = share + group * t
        for a in range(2):
            for r in range(1, group):
                other = peer(r)[0] + group * t
                landed(kv.at[a, other], kv_recv.at[a, other])
            landed(qg.at[a, t], qg_recv.at[a, t])
        query, grad = qg[0, t], qg[1, t]

        def score(j, row_max):
            s = contract(kv[0, j], query, 1, 1) * scale
            probs[j] = contract(kv[1, j], grad, 1, 1)
            ahead = (slab - j) * rows
            higher = jnp.int32(0)
            for l in range(1, level_count):
                higher += jnp.where((slab >> l) != (j >> l), 1, 0)
            distance = (
                lax.broadcasted_iota(jnp.int32, (rows, rows), 1)
                - lax.broadcasted_iota(jnp.int32, (rows, rows), 0)
                + ahead
            )
            near = jnp.where(distance < WINDOW, 1.0, 0.0)
            count = near + jnp.maximum(level[...] - higher.astype(jnp.float32), 0.0)
            count = jnp.where(distance >= 0, count, 0.0)
            s = jnp.where(count > 0.0, s + jnp.log(count), MASKED)
            scores[j] = s
            return jnp.maximum(row_max, jnp.max(s, axis=0, keepdims=True))

        blocks = group * (t + 1)
        row_max = lax.fori_loop(0, blocks, score, jnp.full((1, rows), MASKED, jnp.float32))

        def soften(j, carry):
            row_sum, row_dot = carry
            e = jnp.exp(scores[j] - row_max)
            scores[j] = e
            row_sum += jnp.sum(e, axis=0, keepdims=True)
            row_dot += jnp.sum(e * probs[j], axis=0, keepdims=True)
            return row_sum, row_dot

        zero = jnp.zeros((1, rows), jnp.float32)
        row_sum, row_dot = lax.fori_loop(0, blocks, soften, (zero, zero))
        inverse = 1.0 / row_sum
        grad_dot = row_dot * inverse

        def differentiate(j, dq):
            p = scores[j] * inverse
            ds = (p * (probs[j] - grad_dot)).astype(jnp.bfloat16)
            total[1, j] += contract(p.astype(jnp.bfloat16), grad, 1, 0)
            total[0, j] += contract(ds, query, 1, 0)
            return dq + contract(kv[0, j], ds, 0, 0)

        dq = lax.fori_loop(0, blocks, differentiate, jnp.zeros((width, rows), jnp.float32))
        dq_out[t] = (dq * scale).T.astype(jnp.bfloat16)
        move(*outward(0, t))

    for t in range(slots):
        work(t)

    factors = (scale, 1.0)

    def partial_sum(a, t, r):
        other, place = peer(r)
        return remote(
            part_out.at[r - 1, a, t],
            part_in.at[r - 1, a, t],
            part_send.at[r - 1, a, t],
            part_recv.at[r - 1, a, t],
            place,
        )

    for r in range(1, group):
        for t in range(slots):
            for a in range(2):
                value = total[a, peer(r)[0] + group * t] * factors[a]
                part_out[r - 1, a, t] = value.astype(jnp.bfloat16)
                partial_sum(a, t, r).start()
    for t in range(slots):
        for a in range(2):
            value = total[a, share + group * t] * factors[a]
            for r in range(1, group):
                partial_sum(a, t, r).wait_recv()
                value += part_in[r - 1, a, t].astype(jnp.float32)
            kv_out[a, t] = value.astype(jnp.bfloat16)
            move(*outward(a + 1, t))

    for a, ref in enumerate((dq_ref, dk_ref, dv_ref)):
        for h in range(heads):
            landed(ref.at[:, pl.ds(h * width, width)], out_recv.at[a, h])
        for t in range(slots):
            sent(*outward(a, t))
    for a in range(4):
        for h in range(heads):
            sent(*inward(a, h))
    for a in range(2):
        for t in range(slots):
            for r in range(1, group):
                shared(a, t, r).wait_send()
                partial_sum(a, t, r).wait_send()


def body(devices, batches, query_states, key_states, value_states, out_grad, head_offsets):
    rows, heads = query_states.shape[0], head_offsets.shape[0]
    width = query_states.shape[1] // heads
    group = devices // heads
    slots = devices // group
    half, full = jnp.bfloat16, jnp.float32
    anywhere = pl.BlockSpec(memory_space=pl.ANY)
    dma = pltpu.SemaphoreType.DMA
    result = jax.ShapeDtypeStruct(query_states.shape, half)
    return pl.pallas_call(
        functools.partial(kernel, devices, batches, heads),
        out_shape=(result,) * 3,
        in_specs=[pl.BlockSpec(memory_space=pltpu.SMEM)] + [anywhere] * 4,
        out_specs=(anywhere,) * 3,
        scratch_shapes=[
            pltpu.VMEM((2, devices, rows, width), half),
            pltpu.VMEM((2, slots, rows, width), half),
            pltpu.VMEM((devices, rows, rows), full),
            pltpu.VMEM((devices, rows, rows), full),
            pltpu.VMEM((rows, rows), full),
            pltpu.VMEM((2, devices, rows, width), full),
            pltpu.VMEM((slots, rows, width), half),
            pltpu.VMEM((group - 1, 2, slots, rows, width), half),
            pltpu.VMEM((group - 1, 2, slots, rows, width), half),
            pltpu.VMEM((2, slots, rows, width), half),
            dma((4, heads)),
            dma((2, devices)),
            dma((2, slots)),
            dma((group - 1, 2, slots)),
            dma((group - 1, 2, slots)),
            dma((group - 1, 2, slots)),
            dma((3, slots)),
            dma((3, heads)),
        ],
        compiler_params=pltpu.CompilerParams(
            collective_id=0, has_side_effects=True, vmem_limit_bytes=56 * 2**20
        ),
    )(head_offsets, key_states, value_states, query_states, out_grad)


def solution(mesh):
    slab = P(("batch", "seq"), "head")
    return jax.shard_map(
        functools.partial(body, mesh.shape["seq"], mesh.shape["batch"]),
        mesh=mesh,
        in_specs=(slab,) * 4 + (P("head"),),
        out_specs=(slab,) * 3,
        check_vma=False,
    )
```

```python
import functools

import jax
import jax.numpy as jnp
from jax import lax
from jax.experimental import pallas as pl
from jax.experimental.pallas import tpu as pltpu
from jax.sharding import PartitionSpec as P

WINDOW = 1024
MASKED = -1e30


def contract(left, right, left_dim, right_dim):
    return lax.dot_general(
        left, right, (((left_dim,), (right_dim,)), ((), ())), preferred_element_type=jnp.float32
    )


def kernel(
    devices,
    batches,
    heads,
    off_ref,
    key_ref,
    value_ref,
    query_ref,
    grad_ref,
    dq_ref,
    dk_ref,
    dv_ref,
    kv,
    qg,
    scores,
    probs,
    tops,
    level,
    total,
    dq_out,
    part_out,
    part_in,
    kv_out,
    in_send,
    kv_recv,
    qg_recv,
    peer_send,
    part_send,
    part_recv,
    out_send,
    out_recv,
):
    rows, width = query_ref.shape[0], query_ref.shape[1] // heads
    spots = devices // (heads * batches)
    group = spots * batches
    slots = devices // group
    level_count = devices.bit_length() - 1
    scale = width ** (-0.5)

    seq, batch = lax.axis_index("seq"), lax.axis_index("batch")
    unit = seq // spots
    head, sequence = unit // batches, unit % batches
    share = (seq % spots) * batches + batch
    home_share, home_slot = seq % group, seq // group
    at_home = (sequence == batch) & (home_share == share)

    def worker(h):
        place = {"seq": (h * batches + batch) * spots + home_share // batches}
        place["batch"] = home_share % batches
        return place, at_home & (head == h)

    def owner(t):
        return {"seq": share + group * t, "batch": sequence}, at_home & (home_slot == t)

    def peer(r):
        other = (share + r) % group
        return other, {"seq": unit * spots + other // batches, "batch": other % batches}

    def remote(src, dst, send_sem, recv_sem, place):
        return pltpu.make_async_remote_copy(
            src_ref=src,
            dst_ref=dst,
            send_sem=send_sem,
            recv_sem=recv_sem,
            device_id=place,
            device_id_type=pl.DeviceIdType.MESH,
        )

    def move(src, dst, send_sem, recv_sem, place, same):
        @pl.when(same)
        def _():
            pltpu.make_async_copy(src, dst, recv_sem).start()

        @pl.when(jnp.logical_not(same))
        def _():
            remote(src, dst, send_sem, recv_sem, place).start()

    def sent(src, dst, send_sem, recv_sem, place, same):
        @pl.when(jnp.logical_not(same))
        def _():
            remote(src, dst, send_sem, recv_sem, place).wait_send()

    def landed(ref, sem):
        pltpu.make_async_copy(ref, ref, sem).wait()

    barrier = pltpu.get_barrier_semaphore()

    def greet(place):
        pl.semaphore_signal(barrier, inc=1, device_id=place, device_id_type=pl.DeviceIdType.MESH)

    for place, same in [worker(h) for h in range(heads)] + [owner(t) for t in range(slots)]:
        pl.when(jnp.logical_not(same))(functools.partial(greet, place))
    for r in range(1, group):
        greet(peer(r)[1])
    own = jnp.where(at_home, 1, 0)
    pl.semaphore_wait(barrier, heads + slots - 2 * own + group - 1)

    def inward(a, h):
        source = (key_ref, value_ref, query_ref, grad_ref)[a]
        src = source.at[:, pl.ds(pl.multiple_of(h * width, width), width)]
        if a < 2:
            dst, recv = kv.at[a, seq], kv_recv.at[a, seq]
        else:
            dst, recv = qg.at[a - 2, home_slot], qg_recv.at[a - 2, home_slot]
        return (src, dst, in_send.at[a, h], recv) + worker(h)

    upward = head * 2 < heads

    def far_first(step, count):
        return jnp.where(upward, count - 1 - step, step)

    for step in range(heads):
        for a in range(4):
            move(*inward(a, far_first(step, heads)))

    offset = off_ref[head]
    key_row = lax.broadcasted_iota(jnp.int32, (rows, rows), 0)
    query_row = lax.broadcasted_iota(jnp.int32, (rows, rows), 1)
    apart = (key_row ^ offset) | (query_row ^ offset)
    matched = jnp.zeros((rows, rows), jnp.float32)
    for l in range(1, level_count + 1):
        matched += jnp.where(apart & (2**l - 1) == 0, 1.0, 0.0)
    level[...] = matched

    def clear(j, _):
        total[0, j] = jnp.zeros((rows, width), jnp.float32)
        total[1, j] = jnp.zeros((rows, width), jnp.float32)
        return 0

    lax.fori_loop(0, devices, clear, 0)

    def shared(a, t, r):
        slab = share + group * t
        block = kv.at[a, slab]
        return remote(block, block, peer_send.at[r - 1, a, t], kv_recv.at[a, slab], peer(r)[1])

    def share_out(t):
        for a in range(2):
            slab = share + group * t
            landed(kv.at[a, slab], kv_recv.at[a, slab])
            for r in range(1, group):
                shared(a, t, r).start()

    def outward(a, t):
        src = dq_out.at[t] if a == 0 else kv_out.at[a - 1, t]
        dst = (dq_ref, dk_ref, dv_ref)[a].at[:, pl.ds(pl.multiple_of(head * width, width), width)]
        return (src, dst, out_send.at[a, t], out_recv.at[a, head]) + owner(t)

    def work(t):
        slab = share + group * t
        for a in range(2):
            for r in range(1, group):
                other = peer(r)[0] + group * t
                landed(kv.at[a, other], kv_recv.at[a, other])
            landed(qg.at[a, t], qg_recv.at[a, t])
        query, grad = qg[0, t], qg[1, t]

        def score(j, carry):
            row_max, row_sum, row_dot = carry
            s = contract(kv[0, j], query, 1, 1) * scale
            grad_probs = contract(kv[1, j], grad, 1, 1)
            ahead = (slab - j) * rows
            higher = jnp.int32(0)
            for l in range(1, level_count):
                higher += jnp.where((slab >> l) != (j >> l), 1, 0)
            distance = (
                lax.broadcasted_iota(jnp.int32, (rows, rows), 1)
                - lax.broadcasted_iota(jnp.int32, (rows, rows), 0)
                + ahead
            )
            near = jnp.where(distance < WINDOW, 1.0, 0.0)
            count = near + jnp.maximum(level[...] - higher.astype(jnp.float32), 0.0)
            count = jnp.where(distance >= 0, count, 0.0)
            s = jnp.where(count > 0.0, s, MASKED)
            top = jnp.maximum(row_max, jnp.max(s, axis=0, keepdims=True))
            fade = jnp.exp(row_max - top)
            e = count * jnp.exp(s - top)
            scores[j] = e
            probs[j] = grad_probs
            tops[j] = top
            row_sum = row_sum * fade + jnp.sum(e, axis=0, keepdims=True)
            row_dot = row_dot * fade + jnp.sum(e * grad_probs, axis=0, keepdims=True)
            return top, row_sum, row_dot

        blocks = group * (t + 1)
        zero = jnp.zeros((1, rows), jnp.float32)
        start = (jnp.full((1, rows), MASKED, jnp.float32), zero, zero)
        row_max, row_sum, row_dot = lax.fori_loop(0, blocks, score, start, unroll=2)
        inverse = 1.0 / row_sum
        grad_dot = row_dot * inverse

        def differentiate(j, dq):
            p = scores[j] * (jnp.exp(tops[j] - row_max) * inverse)
            ds = (p * (probs[j] - grad_dot)).astype(jnp.bfloat16)
            total[1, j] += contract(p.astype(jnp.bfloat16), grad, 1, 0)
            total[0, j] += contract(ds, query, 1, 0)
            return dq + contract(kv[0, j], ds, 0, 0)

        dq = jnp.zeros((width, rows), jnp.float32)
        if t < slots - 1:
            share_out(t + 1)
            dq = lax.fori_loop(0, blocks, differentiate, dq, unroll=2)
        else:
            for step in range(slots):
                j = far_first(step, slots)
                dq = lax.fori_loop(
                    0, group, lambda i, dq: differentiate(j * group + i, dq), dq, unroll=2
                )
                swap(j)
                if step > 0:
                    settle(far_first(step - 1, slots))
        dq_out[t] = (dq * scale).T.astype(jnp.bfloat16)
        move(*outward(0, t))

    factors = (scale, 1.0)

    def partial_sum(a, t, r):
        return remote(
            part_out.at[r - 1, a, t],
            part_in.at[r - 1, a, t],
            part_send.at[r - 1, a, t],
            part_recv.at[r - 1, a, t],
            peer(r)[1],
        )

    def swap(t):
        for r in range(1, group):
            for a in range(2):
                value = total[a, peer(r)[0] + group * t] * factors[a]
                part_out[r - 1, a, t] = value.astype(jnp.bfloat16)
                partial_sum(a, t, r).start()

    def settle(t):
        for a in range(2):
            value = total[a, share + group * t] * factors[a]
            for r in range(1, group):
                partial_sum(a, t, r).wait_recv()
                value += part_in[r - 1, a, t].astype(jnp.float32)
            kv_out[a, t] = value.astype(jnp.bfloat16)
            move(*outward(a + 1, t))

    share_out(0)
    for t in range(slots):
        work(t)
    settle(far_first(slots - 1, slots))

    for a, ref in enumerate((dq_ref, dk_ref, dv_ref)):
        for h in range(heads):
            landed(ref.at[:, pl.ds(h * width, width)], out_recv.at[a, h])
        for t in range(slots):
            sent(*outward(a, t))
    for a in range(4):
        for h in range(heads):
            sent(*inward(a, h))
    for a in range(2):
        for t in range(slots):
            for r in range(1, group):
                shared(a, t, r).wait_send()
                partial_sum(a, t, r).wait_send()


def hand_over(*refs):
    copies = [pltpu.make_async_copy(refs[a], refs[a + 3], refs[6].at[a]) for a in range(3)]
    for copy in copies:
        copy.start()
    for copy in copies:
        copy.wait()


def body(devices, batches, query_states, key_states, value_states, out_grad, head_offsets):
    rows, heads = query_states.shape[0], head_offsets.shape[0]
    width = query_states.shape[1] // heads
    group = devices // heads
    slots = devices // group
    half, full = jnp.bfloat16, jnp.float32
    anywhere = pl.BlockSpec(memory_space=pl.ANY)
    dma = pltpu.SemaphoreType.DMA
    result = jax.ShapeDtypeStruct(query_states.shape, half)
    landed = pl.pallas_call(
        functools.partial(kernel, devices, batches, heads),
        out_shape=(result,) * 3,
        in_specs=[pl.BlockSpec(memory_space=pltpu.SMEM)] + [anywhere] * 4,
        out_specs=(anywhere,) * 3,
        scratch_shapes=[
            pltpu.VMEM((2, devices, rows, width), half),
            pltpu.VMEM((2, slots, rows, width), half),
            pltpu.VMEM((devices, rows, rows), full),
            pltpu.VMEM((devices, rows, rows), full),
            pltpu.VMEM((devices, 1, rows), full),
            pltpu.VMEM((rows, rows), full),
            pltpu.VMEM((2, devices, rows, width), full),
            pltpu.VMEM((slots, rows, width), half),
            pltpu.VMEM((group - 1, 2, slots, rows, width), half),
            pltpu.VMEM((group - 1, 2, slots, rows, width), half),
            pltpu.VMEM((2, slots, rows, width), half),
            dma((4, heads)),
            dma((2, devices)),
            dma((2, slots)),
            dma((group - 1, 2, slots)),
            dma((group - 1, 2, slots)),
            dma((group - 1, 2, slots)),
            dma((3, slots)),
            dma((3, heads)),
        ],
        compiler_params=pltpu.CompilerParams(
            collective_id=0, has_side_effects=True, vmem_limit_bytes=56 * 2**20
        ),
    )(head_offsets, key_states, value_states, query_states, out_grad)
    return pl.pallas_call(
        hand_over,
        out_shape=(result,) * 3,
        in_specs=[anywhere] * 3,
        out_specs=(anywhere,) * 3,
        scratch_shapes=[dma((3,))],
    )(*landed)


def solution(mesh):
    slab = P(("batch", "seq"), "head")
    return jax.shard_map(
        functools.partial(body, mesh.shape["seq"], mesh.shape["batch"]),
        mesh=mesh,
        in_specs=(slab,) * 4 + (P("head"),),
        out_specs=(slab,) * 3,
        check_vma=False,
    )
```

```python
import functools

import jax
import jax.numpy as jnp
from jax import lax
from jax.experimental import pallas as pl
from jax.experimental.pallas import tpu as pltpu
from jax.sharding import PartitionSpec as P

WINDOW = 1024
MASKED = -1e30


def contract(left, right, left_dim, right_dim):
    return lax.dot_general(
        left, right, (((left_dim,), (right_dim,)), ((), ())), preferred_element_type=jnp.float32
    )


def kernel(
    devices,
    batches,
    heads,
    off_ref,
    key_ref,
    value_ref,
    query_ref,
    grad_ref,
    dq_ref,
    dk_ref,
    dv_ref,
    kv,
    qg,
    scores,
    probs,
    tops,
    level,
    total,
    dq_out,
    part_out,
    part_in,
    kv_out,
    in_send,
    kv_recv,
    qg_recv,
    peer_send,
    part_send,
    part_recv,
    out_send,
    out_recv,
):
    rows, width = query_ref.shape[0], query_ref.shape[1] // heads
    spots = devices // (heads * batches)
    group = spots * batches
    slots = devices // group
    level_count = devices.bit_length() - 1
    scale = width ** (-0.5)

    seq, batch = lax.axis_index("seq"), lax.axis_index("batch")
    unit = seq // spots
    head, sequence = unit // batches, unit % batches
    share = (seq % spots) * batches + batch
    home_share, home_slot = seq % group, seq // group
    at_home = (sequence == batch) & (home_share == share)

    def worker(h):
        place = {"seq": (h * batches + batch) * spots + home_share // batches}
        place["batch"] = home_share % batches
        return place, at_home & (head == h)

    def owner(t):
        return {"seq": share + group * t, "batch": sequence}, at_home & (home_slot == t)

    def peer(r):
        other = (share + r) % group
        return other, {"seq": unit * spots + other // batches, "batch": other % batches}

    def remote(src, dst, send_sem, recv_sem, place):
        return pltpu.make_async_remote_copy(
            src_ref=src,
            dst_ref=dst,
            send_sem=send_sem,
            recv_sem=recv_sem,
            device_id=place,
            device_id_type=pl.DeviceIdType.MESH,
        )

    def move(src, dst, send_sem, recv_sem, place, same):
        @pl.when(same)
        def _():
            pltpu.make_async_copy(src, dst, recv_sem).start()

        @pl.when(jnp.logical_not(same))
        def _():
            remote(src, dst, send_sem, recv_sem, place).start()

    def sent(src, dst, send_sem, recv_sem, place, same):
        @pl.when(jnp.logical_not(same))
        def _():
            remote(src, dst, send_sem, recv_sem, place).wait_send()

    def landed(ref, sem):
        pltpu.make_async_copy(ref, ref, sem).wait()

    barrier = pltpu.get_barrier_semaphore()

    def greet(place):
        pl.semaphore_signal(barrier, inc=1, device_id=place, device_id_type=pl.DeviceIdType.MESH)

    for place, same in [worker(h) for h in range(heads)] + [owner(t) for t in range(slots)]:
        pl.when(jnp.logical_not(same))(functools.partial(greet, place))
    for r in range(1, group):
        greet(peer(r)[1])
    own = jnp.where(at_home, 1, 0)
    pl.semaphore_wait(barrier, heads + slots - 2 * own + group - 1)

    def inward(a, h):
        source = (key_ref, value_ref, query_ref, grad_ref)[a]
        src = source.at[:, pl.ds(pl.multiple_of(h * width, width), width)]
        if a < 2:
            dst, recv = kv.at[a, seq], kv_recv.at[a, seq]
        else:
            dst, recv = qg.at[a - 2, home_slot], qg_recv.at[a - 2, home_slot]
        return (src, dst, in_send.at[a, h], recv) + worker(h)

    upward = head * 2 < heads

    def far_first(step, count):
        return jnp.where(upward, count - 1 - step, step)

    for step in range(heads):
        for a in range(4):
            move(*inward(a, far_first(step, heads)))

    offset = off_ref[head]
    key_row = lax.broadcasted_iota(jnp.int32, (rows, rows), 0)
    query_row = lax.broadcasted_iota(jnp.int32, (rows, rows), 1)
    apart = (key_row ^ offset) | (query_row ^ offset)
    matched = jnp.zeros((rows, rows), jnp.float32)
    for l in range(1, level_count + 1):
        matched += jnp.where(apart & (2**l - 1) == 0, 1.0, 0.0)
    level[...] = matched

    def clear(j, _):
        total[0, j] = jnp.zeros((rows, width), jnp.float32)
        total[1, j] = jnp.zeros((rows, width), jnp.float32)
        return 0

    lax.fori_loop(0, devices, clear, 0)

    def shared(a, t, r):
        slab = share + group * t
        block = kv.at[a, slab]
        return remote(block, block, peer_send.at[r - 1, a, t], kv_recv.at[a, slab], peer(r)[1])

    def share_out(t):
        for a in range(2):
            slab = share + group * t
            landed(kv.at[a, slab], kv_recv.at[a, slab])
            for r in range(1, group):
                shared(a, t, r).start()

    def outward(a, t):
        src = dq_out.at[t] if a == 0 else kv_out.at[a - 1, t]
        dst = (dq_ref, dk_ref, dv_ref)[a].at[:, pl.ds(pl.multiple_of(head * width, width), width)]
        return (src, dst, out_send.at[a, t], out_recv.at[a, head]) + owner(t)

    def work(t):
        slab = share + group * t
        for a in range(2):
            for r in range(1, group):
                other = peer(r)[0] + group * t
                landed(kv.at[a, other], kv_recv.at[a, other])
            landed(qg.at[a, t], qg_recv.at[a, t])
        query, grad = qg[0, t], qg[1, t]

        def score(j, carry):
            row_max, row_sum, row_dot = carry
            s = contract(kv[0, j], query, 1, 1) * scale
            grad_probs = contract(kv[1, j], grad, 1, 1)
            ahead = (slab - j) * rows
            higher = jnp.int32(0)
            for l in range(1, level_count):
                higher += jnp.where((slab >> l) != (j >> l), 1, 0)
            distance = (
                lax.broadcasted_iota(jnp.int32, (rows, rows), 1)
                - lax.broadcasted_iota(jnp.int32, (rows, rows), 0)
                + ahead
            )
            near = jnp.where(distance < WINDOW, 1.0, 0.0)
            count = near + jnp.maximum(level[...] - higher.astype(jnp.float32), 0.0)
            count = jnp.where(distance >= 0, count, 0.0)
            s = jnp.where(count > 0.0, s, MASKED)
            top = jnp.maximum(row_max, jnp.max(s, axis=0, keepdims=True))
            fade = jnp.exp(row_max - top)
            e = count * jnp.exp(s - top)
            scores[j] = e
            probs[j] = grad_probs
            tops[j] = top
            row_sum = row_sum * fade + jnp.sum(e, axis=0, keepdims=True)
            row_dot = row_dot * fade + jnp.sum(e * grad_probs, axis=0, keepdims=True)
            return top, row_sum, row_dot

        blocks = group * (t + 1)
        zero = jnp.zeros((1, rows), jnp.float32)
        start = (jnp.full((1, rows), MASKED, jnp.float32), zero, zero)
        row_max, row_sum, row_dot = lax.fori_loop(0, blocks, score, start, unroll=2)
        inverse = 1.0 / row_sum
        grad_dot = row_dot * inverse

        def differentiate(j, dq):
            p = scores[j] * (jnp.exp(tops[j] - row_max) * inverse)
            ds = (p * (probs[j] - grad_dot)).astype(jnp.bfloat16)
            total[1, j] += contract(p.astype(jnp.bfloat16), grad, 1, 0)
            total[0, j] += contract(ds, query, 1, 0)
            return dq + contract(kv[0, j], ds, 0, 0)

        dq = jnp.zeros((width, rows), jnp.float32)
        if t < slots - 1:
            share_out(t + 1)
            dq = lax.fori_loop(0, blocks, differentiate, dq, unroll=2)
        else:
            for step in range(slots):
                j = far_first(step, slots)
                dq = lax.fori_loop(
                    0, group, lambda i, dq: differentiate(j * group + i, dq), dq, unroll=2
                )
                swap(j)
                if step > 0:
                    settle(far_first(step - 1, slots))
        dq_out[t] = (dq * scale).T.astype(jnp.bfloat16)
        move(*outward(0, t))

    factors = (scale, 1.0)

    def partial_sum(a, t, r):
        return remote(
            part_out.at[r - 1, a, t],
            part_in.at[r - 1, a, t],
            part_send.at[r - 1, a, t],
            part_recv.at[r - 1, a, t],
            peer(r)[1],
        )

    def swap(t):
        for r in range(1, group):
            for a in range(2):
                value = total[a, peer(r)[0] + group * t] * factors[a]
                part_out[r - 1, a, t] = value.astype(jnp.bfloat16)
                partial_sum(a, t, r).start()

    def settle(t):
        for a in range(2):
            value = total[a, share + group * t] * factors[a]
            for r in range(1, group):
                partial_sum(a, t, r).wait_recv()
                value += part_in[r - 1, a, t].astype(jnp.float32)
            kv_out[a, t] = value.astype(jnp.bfloat16)
            move(*outward(a + 1, t))

    share_out(0)
    for t in range(slots):
        work(t)
    settle(far_first(slots - 1, slots))

    for a, ref in enumerate((dq_ref, dk_ref, dv_ref)):
        for h in range(heads):
            landed(ref.at[:, pl.ds(h * width, width)], out_recv.at[a, h])
        for t in range(slots):
            sent(*outward(a, t))
    for a in range(4):
        for h in range(heads):
            sent(*inward(a, h))
    for a in range(2):
        for t in range(slots):
            for r in range(1, group):
                shared(a, t, r).wait_send()
                partial_sum(a, t, r).wait_send()


def hand_over(*refs):
    for source, target in zip(refs[:3], refs[3:]):
        target[...] = source[...]


def body(devices, batches, query_states, key_states, value_states, out_grad, head_offsets):
    rows, heads = query_states.shape[0], head_offsets.shape[0]
    width = query_states.shape[1] // heads
    group = devices // heads
    slots = devices // group
    half, full = jnp.bfloat16, jnp.float32
    anywhere = pl.BlockSpec(memory_space=pl.ANY)
    dma = pltpu.SemaphoreType.DMA
    result = jax.ShapeDtypeStruct(query_states.shape, half)
    landed = pl.pallas_call(
        functools.partial(kernel, devices, batches, heads),
        out_shape=(result,) * 3,
        in_specs=[pl.BlockSpec(memory_space=pltpu.SMEM)] + [anywhere] * 4,
        out_specs=(anywhere,) * 3,
        scratch_shapes=[
            pltpu.VMEM((2, devices, rows, width), half),
            pltpu.VMEM((2, slots, rows, width), half),
            pltpu.VMEM((devices, rows, rows), full),
            pltpu.VMEM((devices, rows, rows), full),
            pltpu.VMEM((devices, 1, rows), full),
            pltpu.VMEM((rows, rows), full),
            pltpu.VMEM((2, devices, rows, width), full),
            pltpu.VMEM((slots, rows, width), half),
            pltpu.VMEM((group - 1, 2, slots, rows, width), half),
            pltpu.VMEM((group - 1, 2, slots, rows, width), half),
            pltpu.VMEM((2, slots, rows, width), half),
            dma((4, heads)),
            dma((2, devices)),
            dma((2, slots)),
            dma((group - 1, 2, slots)),
            dma((group - 1, 2, slots)),
            dma((group - 1, 2, slots)),
            dma((3, slots)),
            dma((3, heads)),
        ],
        compiler_params=pltpu.CompilerParams(
            collective_id=0, has_side_effects=True, vmem_limit_bytes=56 * 2**20
        ),
    )(head_offsets, key_states, value_states, query_states, out_grad)
    return pl.pallas_call(hand_over, out_shape=(result,) * 3)(*landed)


def solution(mesh):
    slab = P(("batch", "seq"), "head")
    return jax.shard_map(
        functools.partial(body, mesh.shape["seq"], mesh.shape["batch"]),
        mesh=mesh,
        in_specs=(slab,) * 4 + (P("head"),),
        out_specs=(slab,) * 3,
        check_vma=False,
    )
```

```python
import functools

import jax
import jax.numpy as jnp
from jax import lax
from jax.experimental import pallas as pl
from jax.experimental.pallas import tpu as pltpu
from jax.sharding import PartitionSpec as P

WINDOW = 1024
MASKED = -1e30


def contract(left, right, left_dim, right_dim):
    return lax.dot_general(
        left, right, (((left_dim,), (right_dim,)), ((), ())), preferred_element_type=jnp.float32
    )


def kernel(
    devices,
    batches,
    heads,
    off_ref,
    key_ref,
    value_ref,
    query_ref,
    grad_ref,
    dq_ref,
    dk_ref,
    dv_ref,
    kv,
    qg,
    scores,
    tops,
    stats,
    dq_sum,
    level,
    total,
    dq_out,
    part_out,
    part_in,
    kv_out,
    in_send,
    kv_recv,
    qg_recv,
    peer_send,
    part_send,
    part_recv,
    out_send,
    out_recv,
):
    rows, width = query_ref.shape[0], query_ref.shape[1] // heads
    spots = devices // (heads * batches)
    group = spots * batches
    slots = devices // group
    level_count = devices.bit_length() - 1
    scale = width ** (-0.5)

    seq, batch = lax.axis_index("seq"), lax.axis_index("batch")
    unit = seq // spots
    head, sequence = unit // batches, unit % batches
    share = (seq % spots) * batches + batch
    home_share, home_slot = seq % group, seq // group
    at_home = (sequence == batch) & (home_share == share)

    def worker(h):
        place = {"seq": (h * batches + batch) * spots + home_share // batches}
        place["batch"] = home_share % batches
        return place, at_home & (head == h)

    def owner(t):
        return {"seq": share + group * t, "batch": sequence}, at_home & (home_slot == t)

    def peer(r):
        other = (share + r) % group
        return other, {"seq": unit * spots + other // batches, "batch": other % batches}

    def remote(src, dst, send_sem, recv_sem, place):
        return pltpu.make_async_remote_copy(
            src_ref=src,
            dst_ref=dst,
            send_sem=send_sem,
            recv_sem=recv_sem,
            device_id=place,
            device_id_type=pl.DeviceIdType.MESH,
        )

    def move(src, dst, send_sem, recv_sem, place, same):
        @pl.when(same)
        def _():
            pltpu.make_async_copy(src, dst, recv_sem).start()

        @pl.when(jnp.logical_not(same))
        def _():
            remote(src, dst, send_sem, recv_sem, place).start()

    def sent(src, dst, send_sem, recv_sem, place, same):
        @pl.when(jnp.logical_not(same))
        def _():
            remote(src, dst, send_sem, recv_sem, place).wait_send()

    def landed(ref, sem):
        pltpu.make_async_copy(ref, ref, sem).wait()

    barrier = pltpu.get_barrier_semaphore()

    def greet(place):
        pl.semaphore_signal(barrier, inc=1, device_id=place, device_id_type=pl.DeviceIdType.MESH)

    for place, same in [worker(h) for h in range(heads)] + [owner(t) for t in range(slots)]:
        pl.when(jnp.logical_not(same))(functools.partial(greet, place))
    for r in range(1, group):
        greet(peer(r)[1])
    own = jnp.where(at_home, 1, 0)
    pl.semaphore_wait(barrier, heads + slots - 2 * own + group - 1)

    def inward(a, h):
        source = (key_ref, value_ref, query_ref, grad_ref)[a]
        src = source.at[:, pl.ds(pl.multiple_of(h * width, width), width)]
        if a < 2:
            dst, recv = kv.at[a, seq], kv_recv.at[a, seq]
        else:
            dst, recv = qg.at[a - 2, home_slot], qg_recv.at[a - 2, home_slot]
        return (src, dst, in_send.at[a, h], recv) + worker(h)

    upward = home_slot * 2 < slots

    def far_first(step, count):
        return jnp.where(upward, count - 1 - step, step)

    for step in range(heads):
        for a in range(4):
            move(*inward(a, far_first(step, heads)))

    offset = off_ref[head]
    key_row = lax.broadcasted_iota(jnp.int32, (rows, rows), 0)
    query_row = lax.broadcasted_iota(jnp.int32, (rows, rows), 1)
    apart = (key_row ^ offset) | (query_row ^ offset)
    matched = jnp.zeros((rows, rows), jnp.float32)
    for l in range(1, level_count + 1):
        matched += jnp.where(apart & (2**l - 1) == 0, 1.0, 0.0)
    level[...] = matched

    def clear(j, _):
        total[0, j] = jnp.zeros((rows, width), jnp.float32)
        total[1, j] = jnp.zeros((rows, width), jnp.float32)
        return 0

    lax.fori_loop(0, devices, clear, 0)

    for t in range(slots):
        stats[t, 0] = jnp.full((1, rows), MASKED, jnp.float32)
        stats[t, 1] = jnp.zeros((1, rows), jnp.float32)
        stats[t, 2] = jnp.zeros((1, rows), jnp.float32)
        dq_sum[t] = jnp.zeros((width, rows), jnp.float32)

    def near_first(step):
        chosen = jnp.int32(0)
        for base in range(slots):
            nearest = sorted(range(slots), key=lambda t: abs(t - base))
            chosen = jnp.where(home_slot == base, nearest[step], chosen)
        return chosen

    def shared(a, t, r):
        slab = share + group * t
        block = kv.at[a, slab]
        return remote(block, block, peer_send.at[r - 1, a, t], kv_recv.at[a, slab], peer(r)[1])

    def arrive(t):
        for a in range(2):
            slab = share + group * t
            landed(kv.at[a, slab], kv_recv.at[a, slab])
            for r in range(1, group):
                shared(a, t, r).start()
        for a in range(2):
            landed(qg.at[a, t], qg_recv.at[a, t])
        for a in range(2):
            for r in range(1, group):
                other = peer(r)[0] + group * t
                landed(kv.at[a, other], kv_recv.at[a, other])

    def outward(a, t):
        src = dq_out.at[t] if a == 0 else kv_out.at[a - 1, t]
        dst = (dq_ref, dk_ref, dv_ref)[a].at[:, pl.ds(pl.multiple_of(head * width, width), width)]
        return (src, dst, out_send.at[a, t], out_recv.at[a, head]) + owner(t)

    def entry(query_slot, j):
        return group * ((query_slot * (query_slot + 1)) >> 1) + j

    def score_pair(query_slot, key_slot):
        slab = share + group * query_slot
        query, grad = qg[0, query_slot], qg[1, query_slot]

        def score(i, carry):
            row_max, row_sum, row_dot = carry
            j = key_slot * group + i
            s = contract(kv[0, j], query, 1, 1) * scale
            grad_probs = contract(kv[1, j], grad, 1, 1)
            ahead = (slab - j) * rows
            higher = jnp.int32(0)
            for l in range(1, level_count):
                higher += jnp.where((slab >> l) != (j >> l), 1, 0)
            distance = (
                lax.broadcasted_iota(jnp.int32, (rows, rows), 1)
                - lax.broadcasted_iota(jnp.int32, (rows, rows), 0)
                + ahead
            )
            near = jnp.where(distance < WINDOW, 1.0, 0.0)
            count = near + jnp.maximum(level[...] - higher.astype(jnp.float32), 0.0)
            count = jnp.where(distance >= 0, count, 0.0)
            s = jnp.where(count > 0.0, s, MASKED)
            top = jnp.maximum(row_max, jnp.max(s, axis=0, keepdims=True))
            fade = jnp.exp(row_max - top)
            e = count * jnp.exp(s - top)
            scores[entry(query_slot, j)] = e
            tops[entry(query_slot, j)] = top
            row_sum = row_sum * fade + jnp.sum(e, axis=0, keepdims=True)
            row_dot = row_dot * fade + jnp.sum(e * grad_probs, axis=0, keepdims=True)
            return top, row_sum, row_dot

        carry = tuple(stats[query_slot, n] for n in range(3))
        carry = lax.fori_loop(0, group, score, carry, unroll=2)
        for n in range(3):
            stats[query_slot, n] = carry[n]

    def differentiate(query_slot, key_slot):
        query, grad = qg[0, query_slot], qg[1, query_slot]
        row_max = stats[query_slot, 0]
        inverse = 1.0 / stats[query_slot, 1]
        grad_dot = stats[query_slot, 2] * inverse

        def block(i, dq):
            j = key_slot * group + i
            at = entry(query_slot, j)
            p = scores[at] * (jnp.exp(tops[at] - row_max) * inverse)
            grad_probs = contract(kv[1, j], grad, 1, 1)
            ds = (p * (grad_probs - grad_dot)).astype(jnp.bfloat16)
            total[1, j] += contract(p.astype(jnp.bfloat16), grad, 1, 0)
            total[0, j] += contract(ds, query, 1, 0)
            return dq + contract(kv[0, j], ds, 0, 0)

        dq = jnp.zeros((width, rows), jnp.float32)
        dq_sum[query_slot] += lax.fori_loop(0, group, block, dq, unroll=2)

    def finish_query(t):
        dq_out[t] = (dq_sum[t] * scale).T.astype(jnp.bfloat16)
        move(*outward(0, t))

    factors = (scale, 1.0)

    def partial_sum(a, t, r):
        return remote(
            part_out.at[r - 1, a, t],
            part_in.at[r - 1, a, t],
            part_send.at[r - 1, a, t],
            part_recv.at[r - 1, a, t],
            peer(r)[1],
        )

    def swap(t):
        for r in range(1, group):
            for a in range(2):
                value = total[a, peer(r)[0] + group * t] * factors[a]
                part_out[r - 1, a, t] = value.astype(jnp.bfloat16)
                partial_sum(a, t, r).start()

    def settle(t):
        for a in range(2):
            value = total[a, share + group * t] * factors[a]
            for r in range(1, group):
                partial_sum(a, t, r).wait_recv()
                value += part_in[r - 1, a, t].astype(jnp.float32)
            kv_out[a, t] = value.astype(jnp.bfloat16)
            move(*outward(a + 1, t))

    order = [near_first(step) for step in range(slots)]
    for step in range(slots):
        arrive(order[step])
        for other in order[: step + 1]:
            score_pair(jnp.maximum(order[step], other), jnp.minimum(order[step], other))

    for step in range(slots):
        key_slot = far_first(step, slots)

        def one(query_slot, _):
            differentiate(query_slot, key_slot)
            return 0

        lax.fori_loop(key_slot, slots, one, 0)
        swap(key_slot)

        @pl.when(jnp.logical_not(upward))
        def _():
            finish_query(key_slot)

        if step > 0:
            settle(far_first(step - 1, slots))

    @pl.when(upward)
    def _():
        for t in reversed(range(slots)):
            finish_query(t)

    settle(far_first(slots - 1, slots))

    for a, ref in enumerate((dq_ref, dk_ref, dv_ref)):
        for h in range(heads):
            landed(ref.at[:, pl.ds(h * width, width)], out_recv.at[a, h])
        for t in range(slots):
            sent(*outward(a, t))
    for a in range(4):
        for h in range(heads):
            sent(*inward(a, h))
    for a in range(2):
        for t in range(slots):
            for r in range(1, group):
                shared(a, t, r).wait_send()
                partial_sum(a, t, r).wait_send()


def hand_over(*refs):
    for source, target in zip(refs[:3], refs[3:]):
        target[...] = source[...]


def body(devices, batches, query_states, key_states, value_states, out_grad, head_offsets):
    rows, heads = query_states.shape[0], head_offsets.shape[0]
    width = query_states.shape[1] // heads
    group = devices // heads
    slots = devices // group
    entries = group * (slots * (slots + 1) // 2)
    half, full = jnp.bfloat16, jnp.float32
    anywhere = pl.BlockSpec(memory_space=pl.ANY)
    dma = pltpu.SemaphoreType.DMA
    result = jax.ShapeDtypeStruct(query_states.shape, half)
    landed = pl.pallas_call(
        functools.partial(kernel, devices, batches, heads),
        out_shape=(result,) * 3,
        in_specs=[pl.BlockSpec(memory_space=pltpu.SMEM)] + [anywhere] * 4,
        out_specs=(anywhere,) * 3,
        scratch_shapes=[
            pltpu.VMEM((2, devices, rows, width), half),
            pltpu.VMEM((2, slots, rows, width), half),
            pltpu.VMEM((entries, rows, rows), full),
            pltpu.VMEM((entries, 1, rows), full),
            pltpu.VMEM((slots, 3, 1, rows), full),
            pltpu.VMEM((slots, width, rows), full),
            pltpu.VMEM((rows, rows), full),
            pltpu.VMEM((2, devices, rows, width), full),
            pltpu.VMEM((slots, rows, width), half),
            pltpu.VMEM((group - 1, 2, slots, rows, width), half),
            pltpu.VMEM((group - 1, 2, slots, rows, width), half),
            pltpu.VMEM((2, slots, rows, width), half),
            dma((4, heads)),
            dma((2, devices)),
            dma((2, slots)),
            dma((group - 1, 2, slots)),
            dma((group - 1, 2, slots)),
            dma((group - 1, 2, slots)),
            dma((3, slots)),
            dma((3, heads)),
        ],
        compiler_params=pltpu.CompilerParams(
            collective_id=0, has_side_effects=True, vmem_limit_bytes=56 * 2**20
        ),
    )(head_offsets, key_states, value_states, query_states, out_grad)
    return pl.pallas_call(hand_over, out_shape=(result,) * 3)(*landed)


def solution(mesh):
    slab = P(("batch", "seq"), "head")
    return jax.shard_map(
        functools.partial(body, mesh.shape["seq"], mesh.shape["batch"]),
        mesh=mesh,
        in_specs=(slab,) * 4 + (P("head"),),
        out_specs=(slab,) * 3,
        check_vma=False,
    )
```

```python
import functools

import jax
import jax.numpy as jnp
from jax import lax
from jax.experimental import pallas as pl
from jax.experimental.pallas import tpu as pltpu
from jax.sharding import PartitionSpec as P

WINDOW = 1024
MASKED = -1e30


def contract(left, right, left_dim, right_dim):
    return lax.dot_general(
        left, right, (((left_dim,), (right_dim,)), ((), ())), preferred_element_type=jnp.float32
    )


def send_order(count, base):
    upper = base * 2 >= count
    same = [t for t in range(count) if (t * 2 >= count) == upper and t != base]
    cross = [t for t in range(count) if (t * 2 >= count) != upper]
    cross = sorted(cross, key=lambda t: -abs(t - base))
    inner = abs(2 * base + 1 - count) * 2 < count
    return [base] + (same + cross if inner else cross + same)


def arrival_order(count, base):
    def key(t):
        return send_order(count, t).index(base), abs(t - base)

    return sorted(range(count), key=key)


def kernel(
    devices,
    batches,
    heads,
    off_ref,
    key_ref,
    value_ref,
    query_ref,
    grad_ref,
    dq_ref,
    dk_ref,
    dv_ref,
    kv,
    qg,
    scores,
    tops,
    stats,
    dq_sum,
    level,
    total,
    dq_out,
    part_out,
    part_in,
    kv_out,
    in_send,
    kv_recv,
    qg_recv,
    peer_send,
    part_send,
    part_recv,
    out_send,
    out_recv,
):
    rows, width = query_ref.shape[0], query_ref.shape[1] // heads
    spots = devices // (heads * batches)
    group = spots * batches
    slots = devices // group
    level_count = devices.bit_length() - 1
    scale = width ** (-0.5)

    seq, batch = lax.axis_index("seq"), lax.axis_index("batch")
    unit = seq // spots
    head, sequence = unit // batches, unit % batches
    share = (seq % spots) * batches + batch
    home_share, home_slot = seq % group, seq // group
    at_home = (sequence == batch) & (home_share == share)

    def worker(h):
        place = {"seq": (h * batches + batch) * spots + home_share // batches}
        place["batch"] = home_share % batches
        return place, at_home & (head == h)

    def owner(t):
        return {"seq": share + group * t, "batch": sequence}, at_home & (home_slot == t)

    def peer(r):
        other = (share + r) % group
        return other, {"seq": unit * spots + other // batches, "batch": other % batches}

    def remote(src, dst, send_sem, recv_sem, place):
        return pltpu.make_async_remote_copy(
            src_ref=src,
            dst_ref=dst,
            send_sem=send_sem,
            recv_sem=recv_sem,
            device_id=place,
            device_id_type=pl.DeviceIdType.MESH,
        )

    def move(src, dst, send_sem, recv_sem, place, same):
        @pl.when(same)
        def _():
            pltpu.make_async_copy(src, dst, recv_sem).start()

        @pl.when(jnp.logical_not(same))
        def _():
            remote(src, dst, send_sem, recv_sem, place).start()

    def sent(src, dst, send_sem, recv_sem, place, same):
        @pl.when(jnp.logical_not(same))
        def _():
            remote(src, dst, send_sem, recv_sem, place).wait_send()

    def landed(ref, sem):
        pltpu.make_async_copy(ref, ref, sem).wait()

    barrier = pltpu.get_barrier_semaphore()

    def greet(place):
        pl.semaphore_signal(barrier, inc=1, device_id=place, device_id_type=pl.DeviceIdType.MESH)

    for place, same in [worker(h) for h in range(heads)] + [owner(t) for t in range(slots)]:
        pl.when(jnp.logical_not(same))(functools.partial(greet, place))
    for r in range(1, group):
        greet(peer(r)[1])
    own = jnp.where(at_home, 1, 0)
    pl.semaphore_wait(barrier, heads + slots - 2 * own + group - 1)

    def inward(a, h):
        source = (key_ref, value_ref, query_ref, grad_ref)[a]
        src = source.at[:, pl.ds(pl.multiple_of(h * width, width), width)]
        if a < 2:
            dst, recv = kv.at[a, seq], kv_recv.at[a, seq]
        else:
            dst, recv = qg.at[a - 2, home_slot], qg_recv.at[a - 2, home_slot]
        return (src, dst, in_send.at[a, h], recv) + worker(h)

    def ordered(order, count, step):
        chosen = jnp.int32(0)
        for base in range(count):
            chosen = jnp.where(home_slot == base, order(count, base)[step], chosen)
        return chosen

    upward = home_slot * 2 < slots

    def far_first(step, count):
        return jnp.where(upward, count - 1 - step, step)

    for step in range(heads):
        for a in range(4):
            move(*inward(a, ordered(send_order, heads, step)))

    offset = off_ref[head]
    key_row = lax.broadcasted_iota(jnp.int32, (rows, rows), 0)
    query_row = lax.broadcasted_iota(jnp.int32, (rows, rows), 1)
    apart = (key_row ^ offset) | (query_row ^ offset)
    matched = jnp.zeros((rows, rows), jnp.float32)
    for l in range(1, level_count + 1):
        matched += jnp.where(apart & (2**l - 1) == 0, 1.0, 0.0)
    level[...] = matched

    def clear(j, _):
        total[0, j] = jnp.zeros((rows, width), jnp.float32)
        total[1, j] = jnp.zeros((rows, width), jnp.float32)
        return 0

    lax.fori_loop(0, devices, clear, 0)

    for t in range(slots):
        stats[t, 0] = jnp.full((1, rows), MASKED, jnp.float32)
        stats[t, 1] = jnp.zeros((1, rows), jnp.float32)
        stats[t, 2] = jnp.zeros((1, rows), jnp.float32)
        dq_sum[t] = jnp.zeros((width, rows), jnp.float32)

    def shared(a, t, r):
        slab = share + group * t
        block = kv.at[a, slab]
        return remote(block, block, peer_send.at[r - 1, a, t], kv_recv.at[a, slab], peer(r)[1])

    def arrive(t):
        for a in range(2):
            slab = share + group * t
            landed(kv.at[a, slab], kv_recv.at[a, slab])
            for r in range(1, group):
                shared(a, t, r).start()
        for a in range(2):
            landed(qg.at[a, t], qg_recv.at[a, t])
        for a in range(2):
            for r in range(1, group):
                other = peer(r)[0] + group * t
                landed(kv.at[a, other], kv_recv.at[a, other])

    def outward(a, t):
        src = dq_out.at[t] if a == 0 else kv_out.at[a - 1, t]
        dst = (dq_ref, dk_ref, dv_ref)[a].at[:, pl.ds(pl.multiple_of(head * width, width), width)]
        return (src, dst, out_send.at[a, t], out_recv.at[a, head]) + owner(t)

    def entry(query_slot, j):
        return group * ((query_slot * (query_slot + 1)) >> 1) + j

    def score_pair(query_slot, key_slot):
        slab = share + group * query_slot
        query, grad = qg[0, query_slot], qg[1, query_slot]

        def score(i, carry):
            row_max, row_sum, row_dot = carry
            j = key_slot * group + i
            s = contract(kv[0, j], query, 1, 1) * scale
            grad_probs = contract(kv[1, j], grad, 1, 1)
            ahead = (slab - j) * rows
            higher = jnp.int32(0)
            for l in range(1, level_count):
                higher += jnp.where((slab >> l) != (j >> l), 1, 0)
            distance = (
                lax.broadcasted_iota(jnp.int32, (rows, rows), 1)
                - lax.broadcasted_iota(jnp.int32, (rows, rows), 0)
                + ahead
            )
            near = jnp.where(distance < WINDOW, 1.0, 0.0)
            count = near + jnp.maximum(level[...] - higher.astype(jnp.float32), 0.0)
            count = jnp.where(distance >= 0, count, 0.0)
            s = jnp.where(count > 0.0, s, MASKED)
            top = jnp.maximum(row_max, jnp.max(s, axis=0, keepdims=True))
            fade = jnp.exp(row_max - top)
            e = count * jnp.exp(s - top)
            scores[entry(query_slot, j)] = e
            tops[entry(query_slot, j)] = top
            row_sum = row_sum * fade + jnp.sum(e, axis=0, keepdims=True)
            row_dot = row_dot * fade + jnp.sum(e * grad_probs, axis=0, keepdims=True)
            return top, row_sum, row_dot

        carry = tuple(stats[query_slot, n] for n in range(3))
        carry = lax.fori_loop(0, group, score, carry, unroll=2)
        for n in range(3):
            stats[query_slot, n] = carry[n]

    def differentiate(query_slot, key_slot):
        query, grad = qg[0, query_slot], qg[1, query_slot]
        row_max = stats[query_slot, 0]
        inverse = 1.0 / stats[query_slot, 1]
        grad_dot = stats[query_slot, 2] * inverse

        def block(i, dq):
            j = key_slot * group + i
            at = entry(query_slot, j)
            p = scores[at] * (jnp.exp(tops[at] - row_max) * inverse)
            grad_probs = contract(kv[1, j], grad, 1, 1)
            ds = (p * (grad_probs - grad_dot)).astype(jnp.bfloat16)
            total[1, j] += contract(p.astype(jnp.bfloat16), grad, 1, 0)
            total[0, j] += contract(ds, query, 1, 0)
            return dq + contract(kv[0, j], ds, 0, 0)

        dq = jnp.zeros((width, rows), jnp.float32)
        dq_sum[query_slot] += lax.fori_loop(0, group, block, dq, unroll=2)

    def finish_query(t):
        dq_out[t] = (dq_sum[t] * scale).T.astype(jnp.bfloat16)
        move(*outward(0, t))

    factors = (scale, 1.0)

    def partial_sum(a, t, r):
        return remote(
            part_out.at[r - 1, a, t],
            part_in.at[r - 1, a, t],
            part_send.at[r - 1, a, t],
            part_recv.at[r - 1, a, t],
            peer(r)[1],
        )

    def swap(t):
        for r in range(1, group):
            for a in range(2):
                value = total[a, peer(r)[0] + group * t] * factors[a]
                part_out[r - 1, a, t] = value.astype(jnp.bfloat16)
                partial_sum(a, t, r).start()

    def settle(t):
        for a in range(2):
            value = total[a, share + group * t] * factors[a]
            for r in range(1, group):
                partial_sum(a, t, r).wait_recv()
                value += part_in[r - 1, a, t].astype(jnp.float32)
            kv_out[a, t] = value.astype(jnp.bfloat16)
            move(*outward(a + 1, t))

    order = [ordered(arrival_order, slots, step) for step in range(slots)]
    for step in range(slots):
        arrive(order[step])
        for other in order[: step + 1]:
            score_pair(jnp.maximum(order[step], other), jnp.minimum(order[step], other))

    for step in range(slots):
        key_slot = far_first(step, slots)

        def one(query_slot, _):
            differentiate(query_slot, key_slot)
            return 0

        lax.fori_loop(key_slot, slots, one, 0)
        swap(key_slot)

        @pl.when(jnp.logical_not(upward))
        def _():
            finish_query(key_slot)

        if step > 0:
            settle(far_first(step - 1, slots))

    @pl.when(upward)
    def _():
        for t in reversed(range(slots)):
            finish_query(t)

    settle(far_first(slots - 1, slots))

    for a, ref in enumerate((dq_ref, dk_ref, dv_ref)):
        for h in range(heads):
            landed(ref.at[:, pl.ds(h * width, width)], out_recv.at[a, h])
        for t in range(slots):
            sent(*outward(a, t))
    for a in range(4):
        for h in range(heads):
            sent(*inward(a, h))
    for a in range(2):
        for t in range(slots):
            for r in range(1, group):
                shared(a, t, r).wait_send()
                partial_sum(a, t, r).wait_send()


def hand_over(*refs):
    for source, target in zip(refs[:3], refs[3:]):
        target[...] = source[...]


def body(devices, batches, query_states, key_states, value_states, out_grad, head_offsets):
    rows, heads = query_states.shape[0], head_offsets.shape[0]
    width = query_states.shape[1] // heads
    group = devices // heads
    slots = devices // group
    entries = group * (slots * (slots + 1) // 2)
    half, full = jnp.bfloat16, jnp.float32
    anywhere = pl.BlockSpec(memory_space=pl.ANY)
    dma = pltpu.SemaphoreType.DMA
    result = jax.ShapeDtypeStruct(query_states.shape, half)
    landed = pl.pallas_call(
        functools.partial(kernel, devices, batches, heads),
        out_shape=(result,) * 3,
        in_specs=[pl.BlockSpec(memory_space=pltpu.SMEM)] + [anywhere] * 4,
        out_specs=(anywhere,) * 3,
        scratch_shapes=[
            pltpu.VMEM((2, devices, rows, width), half),
            pltpu.VMEM((2, slots, rows, width), half),
            pltpu.VMEM((entries, rows, rows), full),
            pltpu.VMEM((entries, 1, rows), full),
            pltpu.VMEM((slots, 3, 1, rows), full),
            pltpu.VMEM((slots, width, rows), full),
            pltpu.VMEM((rows, rows), full),
            pltpu.VMEM((2, devices, rows, width), full),
            pltpu.VMEM((slots, rows, width), half),
            pltpu.VMEM((group - 1, 2, slots, rows, width), half),
            pltpu.VMEM((group - 1, 2, slots, rows, width), half),
            pltpu.VMEM((2, slots, rows, width), half),
            dma((4, heads)),
            dma((2, devices)),
            dma((2, slots)),
            dma((group - 1, 2, slots)),
            dma((group - 1, 2, slots)),
            dma((group - 1, 2, slots)),
            dma((3, slots)),
            dma((3, heads)),
        ],
        compiler_params=pltpu.CompilerParams(
            collective_id=0, has_side_effects=True, vmem_limit_bytes=56 * 2**20
        ),
    )(head_offsets, key_states, value_states, query_states, out_grad)
    return pl.pallas_call(hand_over, out_shape=(result,) * 3)(*landed)


def solution(mesh):
    slab = P(("batch", "seq"), "head")
    return jax.shard_map(
        functools.partial(body, mesh.shape["seq"], mesh.shape["batch"]),
        mesh=mesh,
        in_specs=(slab,) * 4 + (P("head"),),
        out_specs=(slab,) * 3,
        check_vma=False,
    )
```

```python
import functools

import jax
import jax.numpy as jnp
from jax import lax
from jax.experimental import pallas as pl
from jax.experimental.pallas import tpu as pltpu
from jax.sharding import PartitionSpec as P

WINDOW = 1024
MASKED = -1e30


def contract(left, right, left_dim, right_dim):
    return lax.dot_general(
        left, right, (((left_dim,), (right_dim,)), ((), ())), preferred_element_type=jnp.float32
    )


def kernel(
    devices,
    batches,
    heads,
    off_ref,
    key_ref,
    value_ref,
    query_ref,
    grad_ref,
    dq_ref,
    dk_ref,
    dv_ref,
    kv,
    qg,
    scores,
    probs,
    tops,
    level,
    total,
    dq_out,
    part_out,
    part_in,
    kv_out,
    in_send,
    kv_recv,
    qg_recv,
    peer_send,
    part_send,
    part_recv,
    out_send,
    out_recv,
):
    rows, width = query_ref.shape[0], query_ref.shape[1] // heads
    spots = devices // (heads * batches)
    group = spots * batches
    slots = devices // group
    level_count = devices.bit_length() - 1
    scale = width ** (-0.5)

    seq, batch = lax.axis_index("seq"), lax.axis_index("batch")
    unit = seq // spots
    head, sequence = unit // batches, unit % batches
    share = (seq % spots) * batches + batch
    home_share, home_slot = seq % group, seq // group
    at_home = (sequence == batch) & (home_share == share)

    def worker(h):
        place = {"seq": (h * batches + batch) * spots + home_share // batches}
        place["batch"] = home_share % batches
        return place, at_home & (head == h)

    def owner(t):
        return {"seq": share + group * t, "batch": sequence}, at_home & (home_slot == t)

    def peer(r):
        other = (share + r) % group
        return other, {"seq": unit * spots + other // batches, "batch": other % batches}

    def remote(src, dst, send_sem, recv_sem, place):
        return pltpu.make_async_remote_copy(
            src_ref=src,
            dst_ref=dst,
            send_sem=send_sem,
            recv_sem=recv_sem,
            device_id=place,
            device_id_type=pl.DeviceIdType.MESH,
        )

    def move(src, dst, send_sem, recv_sem, place, same):
        @pl.when(same)
        def _():
            pltpu.make_async_copy(src, dst, recv_sem).start()

        @pl.when(jnp.logical_not(same))
        def _():
            remote(src, dst, send_sem, recv_sem, place).start()

    def sent(src, dst, send_sem, recv_sem, place, same):
        @pl.when(jnp.logical_not(same))
        def _():
            remote(src, dst, send_sem, recv_sem, place).wait_send()

    def landed(ref, sem):
        pltpu.make_async_copy(ref, ref, sem).wait()

    barrier = pltpu.get_barrier_semaphore()

    def greet(place):
        pl.semaphore_signal(barrier, inc=1, device_id=place, device_id_type=pl.DeviceIdType.MESH)

    for place, same in [worker(h) for h in range(heads)] + [owner(t) for t in range(slots)]:
        pl.when(jnp.logical_not(same))(functools.partial(greet, place))
    for r in range(1, group):
        greet(peer(r)[1])
    own = jnp.where(at_home, 1, 0)
    pl.semaphore_wait(barrier, heads + slots - 2 * own + group - 1)

    def inward(a, h):
        source = (key_ref, value_ref, query_ref, grad_ref)[a]
        src = source.at[:, pl.ds(pl.multiple_of(h * width, width), width)]
        if a < 2:
            dst, recv = kv.at[a, seq], kv_recv.at[a, seq]
        else:
            dst, recv = qg.at[a - 2, home_slot], qg_recv.at[a - 2, home_slot]
        return (src, dst, in_send.at[a, h], recv) + worker(h)

    upward = head * 2 < heads

    def far_first(step, count):
        return jnp.where(upward, count - 1 - step, step)

    for step in range(heads):
        for a in range(4):
            move(*inward(a, far_first(step, heads)))

    offset = off_ref[head]
    key_row = lax.broadcasted_iota(jnp.int32, (rows, rows), 0)
    query_row = lax.broadcasted_iota(jnp.int32, (rows, rows), 1)
    apart = (key_row ^ offset) | (query_row ^ offset)
    matched = jnp.zeros((rows, rows), jnp.float32)
    for l in range(1, level_count + 1):
        matched += jnp.where(apart & (2**l - 1) == 0, 1.0, 0.0)
    level[...] = matched

    def clear(j, _):
        total[0, j] = jnp.zeros((rows, width), jnp.float32)
        total[1, j] = jnp.zeros((rows, width), jnp.float32)
        return 0

    lax.fori_loop(0, devices, clear, 0)

    def shared(a, t, r):
        slab = share + group * t
        block = kv.at[a, slab]
        return remote(block, block, peer_send.at[r - 1, a, t], kv_recv.at[a, slab], peer(r)[1])

    def share_out(t):
        for a in range(2):
            slab = share + group * t
            landed(kv.at[a, slab], kv_recv.at[a, slab])
            for r in range(1, group):
                shared(a, t, r).start()

    def outward(a, t):
        src = dq_out.at[t] if a == 0 else kv_out.at[a - 1, t]
        dst = (dq_ref, dk_ref, dv_ref)[a].at[:, pl.ds(pl.multiple_of(head * width, width), width)]
        return (src, dst, out_send.at[a, t], out_recv.at[a, head]) + owner(t)

    def work(t):
        slab = share + group * t
        for a in range(2):
            for r in range(1, group):
                other = peer(r)[0] + group * t
                landed(kv.at[a, other], kv_recv.at[a, other])
            landed(qg.at[a, t], qg_recv.at[a, t])
        query, grad = qg[0, t], qg[1, t]

        def score(key_slot, i, carry):
            j = key_slot * group + i
            closest = group * (t - key_slot) - (group - 1)
            farthest = group * (t - key_slot) + (group - 1)
            row_max, row_sum, row_dot = carry
            s = contract(kv[0, j], query, 1, 1) * scale
            grad_probs = contract(kv[1, j], grad, 1, 1)
            ahead = (slab - j) * rows
            higher = jnp.int32(0)
            for l in range(1, level_count):
                higher += jnp.where((slab >> l) != (j >> l), 1, 0)
            distance = (
                lax.broadcasted_iota(jnp.int32, (rows, rows), 1)
                - lax.broadcasted_iota(jnp.int32, (rows, rows), 0)
                + ahead
            )
            count = jnp.maximum(level[...] - higher.astype(jnp.float32), 0.0)
            inside = (farthest + 1) * rows - 1 < WINDOW
            if inside:
                count += 1.0
            elif (closest - 1) * rows + 1 < WINDOW:
                count += jnp.where(distance < WINDOW, 1.0, 0.0)
            if closest < 1:
                count = jnp.where(distance >= 0, count, 0.0)
            if not inside or closest < 1:
                s = jnp.where(count > 0.0, s, MASKED)
            top = jnp.maximum(row_max, jnp.max(s, axis=0, keepdims=True))
            fade = jnp.exp(row_max - top)
            e = count * jnp.exp(s - top)
            scores[j] = e
            probs[j] = grad_probs
            tops[j] = top
            row_sum = row_sum * fade + jnp.sum(e, axis=0, keepdims=True)
            row_dot = row_dot * fade + jnp.sum(e * grad_probs, axis=0, keepdims=True)
            return top, row_sum, row_dot

        zero = jnp.zeros((1, rows), jnp.float32)
        start = (jnp.full((1, rows), MASKED, jnp.float32), zero, zero)
        for key_slot in range(t + 1):
            start = lax.fori_loop(0, group, functools.partial(score, key_slot), start, unroll=2)
        row_max, row_sum, row_dot = start
        inverse = 1.0 / row_sum
        grad_dot = row_dot * inverse

        def differentiate(j, dq):
            p = scores[j] * (jnp.exp(tops[j] - row_max) * inverse)
            ds = (p * (probs[j] - grad_dot)).astype(jnp.bfloat16)
            total[1, j] += contract(p.astype(jnp.bfloat16), grad, 1, 0)
            total[0, j] += contract(ds, query, 1, 0)
            return dq + contract(kv[0, j], ds, 0, 0)

        dq = jnp.zeros((width, rows), jnp.float32)
        if t < slots - 1:
            share_out(t + 1)
            for key_slot in range(t + 1):
                dq = lax.fori_loop(
                    key_slot * group, (key_slot + 1) * group, differentiate, dq, unroll=2
                )
        else:
            for step in range(slots):
                j = far_first(step, slots)
                dq = lax.fori_loop(
                    0, group, lambda i, dq: differentiate(j * group + i, dq), dq, unroll=2
                )
                swap(j)
                if step > 0:
                    settle(far_first(step - 1, slots))
        dq_out[t] = (dq * scale).T.astype(jnp.bfloat16)
        move(*outward(0, t))

    factors = (scale, 1.0)

    def partial_sum(a, t, r):
        return remote(
            part_out.at[r - 1, a, t],
            part_in.at[r - 1, a, t],
            part_send.at[r - 1, a, t],
            part_recv.at[r - 1, a, t],
            peer(r)[1],
        )

    def swap(t):
        for r in range(1, group):
            for a in range(2):
                value = total[a, peer(r)[0] + group * t] * factors[a]
                part_out[r - 1, a, t] = value.astype(jnp.bfloat16)
                partial_sum(a, t, r).start()

    def settle(t):
        for a in range(2):
            value = total[a, share + group * t] * factors[a]
            for r in range(1, group):
                partial_sum(a, t, r).wait_recv()
                value += part_in[r - 1, a, t].astype(jnp.float32)
            kv_out[a, t] = value.astype(jnp.bfloat16)
            move(*outward(a + 1, t))

    share_out(0)
    for t in range(slots):
        work(t)
    settle(far_first(slots - 1, slots))

    for a, ref in enumerate((dq_ref, dk_ref, dv_ref)):
        for h in range(heads):
            landed(ref.at[:, pl.ds(h * width, width)], out_recv.at[a, h])
        for t in range(slots):
            sent(*outward(a, t))
    for a in range(4):
        for h in range(heads):
            sent(*inward(a, h))
    for a in range(2):
        for t in range(slots):
            for r in range(1, group):
                shared(a, t, r).wait_send()
                partial_sum(a, t, r).wait_send()


def hand_over(*refs):
    for source, target in zip(refs[:3], refs[3:]):
        target[...] = source[...]


def body(devices, batches, query_states, key_states, value_states, out_grad, head_offsets):
    rows, heads = query_states.shape[0], head_offsets.shape[0]
    width = query_states.shape[1] // heads
    group = devices // heads
    slots = devices // group
    half, full = jnp.bfloat16, jnp.float32
    anywhere = pl.BlockSpec(memory_space=pl.ANY)
    dma = pltpu.SemaphoreType.DMA
    result = jax.ShapeDtypeStruct(query_states.shape, half)
    landed = pl.pallas_call(
        functools.partial(kernel, devices, batches, heads),
        out_shape=(result,) * 3,
        in_specs=[pl.BlockSpec(memory_space=pltpu.SMEM)] + [anywhere] * 4,
        out_specs=(anywhere,) * 3,
        scratch_shapes=[
            pltpu.VMEM((2, devices, rows, width), half),
            pltpu.VMEM((2, slots, rows, width), half),
            pltpu.VMEM((devices, rows, rows), full),
            pltpu.VMEM((devices, rows, rows), full),
            pltpu.VMEM((devices, 1, rows), full),
            pltpu.VMEM((rows, rows), full),
            pltpu.VMEM((2, devices, rows, width), full),
            pltpu.VMEM((slots, rows, width), half),
            pltpu.VMEM((group - 1, 2, slots, rows, width), half),
            pltpu.VMEM((group - 1, 2, slots, rows, width), half),
            pltpu.VMEM((2, slots, rows, width), half),
            dma((4, heads)),
            dma((2, devices)),
            dma((2, slots)),
            dma((group - 1, 2, slots)),
            dma((group - 1, 2, slots)),
            dma((group - 1, 2, slots)),
            dma((3, slots)),
            dma((3, heads)),
        ],
        compiler_params=pltpu.CompilerParams(
            collective_id=0, has_side_effects=True, vmem_limit_bytes=56 * 2**20
        ),
    )(head_offsets, key_states, value_states, query_states, out_grad)
    return pl.pallas_call(hand_over, out_shape=(result,) * 3)(*landed)


def solution(mesh):
    slab = P(("batch", "seq"), "head")
    return jax.shard_map(
        functools.partial(body, mesh.shape["seq"], mesh.shape["batch"]),
        mesh=mesh,
        in_specs=(slab,) * 4 + (P("head"),),
        out_specs=(slab,) * 3,
        check_vma=False,
    )
```

```python
import functools

import jax
import jax.numpy as jnp
from jax import lax
from jax.experimental import pallas as pl
from jax.experimental.pallas import tpu as pltpu
from jax.sharding import PartitionSpec as P

WINDOW = 1024
MASKED = -1e30


def contract(left, right, left_dim, right_dim):
    return lax.dot_general(
        left, right, (((left_dim,), (right_dim,)), ((), ())), preferred_element_type=jnp.float32
    )


def kernel(
    devices,
    batches,
    heads,
    off_ref,
    key_ref,
    value_ref,
    query_ref,
    grad_ref,
    dq_ref,
    dk_ref,
    dv_ref,
    kv,
    qg,
    scores,
    probs,
    tops,
    level,
    total,
    dq_out,
    part_out,
    part_in,
    kv_out,
    in_send,
    kv_recv,
    qg_recv,
    peer_send,
    part_send,
    part_recv,
    out_send,
    out_recv,
):
    rows, width = query_ref.shape[0], query_ref.shape[1] // heads
    spots = devices // (heads * batches)
    group = spots * batches
    slots = devices // group
    level_count = devices.bit_length() - 1
    scale = width ** (-0.5)
    step_blocks = 2 if group % 2 == 0 else 1

    seq, batch = lax.axis_index("seq"), lax.axis_index("batch")
    unit = seq // spots
    head, sequence = unit // batches, unit % batches
    share = (seq % spots) * batches + batch
    home_share, home_slot = seq % group, seq // group
    at_home = (sequence == batch) & (home_share == share)

    def worker(h):
        place = {"seq": (h * batches + batch) * spots + home_share // batches}
        place["batch"] = home_share % batches
        return place, at_home & (head == h)

    def owner(t):
        return {"seq": share + group * t, "batch": sequence}, at_home & (home_slot == t)

    def peer(r):
        other = (share + r) % group
        return other, {"seq": unit * spots + other // batches, "batch": other % batches}

    def remote(src, dst, send_sem, recv_sem, place):
        return pltpu.make_async_remote_copy(
            src_ref=src,
            dst_ref=dst,
            send_sem=send_sem,
            recv_sem=recv_sem,
            device_id=place,
            device_id_type=pl.DeviceIdType.MESH,
        )

    def move(src, dst, send_sem, recv_sem, place, same):
        @pl.when(same)
        def _():
            pltpu.make_async_copy(src, dst, recv_sem).start()

        @pl.when(jnp.logical_not(same))
        def _():
            remote(src, dst, send_sem, recv_sem, place).start()

    def sent(src, dst, send_sem, recv_sem, place, same):
        @pl.when(jnp.logical_not(same))
        def _():
            remote(src, dst, send_sem, recv_sem, place).wait_send()

    def landed(ref, sem):
        pltpu.make_async_copy(ref, ref, sem).wait()

    barrier = pltpu.get_barrier_semaphore()

    def greet(place):
        pl.semaphore_signal(barrier, inc=1, device_id=place, device_id_type=pl.DeviceIdType.MESH)

    for place, same in [worker(h) for h in range(heads)] + [owner(t) for t in range(slots)]:
        pl.when(jnp.logical_not(same))(functools.partial(greet, place))
    for r in range(1, group):
        greet(peer(r)[1])
    own = jnp.where(at_home, 1, 0)
    pl.semaphore_wait(barrier, heads + slots - 2 * own + group - 1)

    def inward(a, h):
        source = (key_ref, value_ref, query_ref, grad_ref)[a]
        src = source.at[:, pl.ds(pl.multiple_of(h * width, width), width)]
        if a < 2:
            dst, recv = kv.at[a, seq], kv_recv.at[a, seq]
        else:
            dst, recv = qg.at[a - 2, home_slot], qg_recv.at[a - 2, home_slot]
        return (src, dst, in_send.at[a, h], recv) + worker(h)

    upward = head * 2 < heads

    def far_first(step, count):
        return jnp.where(upward, count - 1 - step, step)

    for step in range(heads):
        for a in range(4):
            move(*inward(a, far_first(step, heads)))

    offset = off_ref[head]
    key_row = lax.broadcasted_iota(jnp.int32, (rows, rows), 0)
    query_row = lax.broadcasted_iota(jnp.int32, (rows, rows), 1)
    apart = (key_row ^ offset) | (query_row ^ offset)
    matched = jnp.zeros((rows, rows), jnp.float32)
    for l in range(1, level_count + 1):
        matched += jnp.where(apart & (2**l - 1) == 0, 1.0, 0.0)
    level[...] = matched

    def clear(j, _):
        total[0, j] = jnp.zeros((rows, width), jnp.float32)
        total[1, j] = jnp.zeros((rows, width), jnp.float32)
        return 0

    lax.fori_loop(0, devices, clear, 0)

    def shared(a, t, r):
        slab = share + group * t
        block = kv.at[a, slab]
        return remote(block, block, peer_send.at[r - 1, a, t], kv_recv.at[a, slab], peer(r)[1])

    def share_out(t):
        for a in range(2):
            slab = share + group * t
            landed(kv.at[a, slab], kv_recv.at[a, slab])
            for r in range(1, group):
                shared(a, t, r).start()

    def outward(a, t):
        src = dq_out.at[t] if a == 0 else kv_out.at[a - 1, t]
        dst = (dq_ref, dk_ref, dv_ref)[a].at[:, pl.ds(pl.multiple_of(head * width, width), width)]
        return (src, dst, out_send.at[a, t], out_recv.at[a, head]) + owner(t)

    def work(t):
        slab = share + group * t
        for a in range(2):
            for r in range(1, group):
                other = peer(r)[0] + group * t
                landed(kv.at[a, other], kv_recv.at[a, other])
            landed(qg.at[a, t], qg_recv.at[a, t])
        query, grad = qg[0, t], qg[1, t]

        def masked(key_slot, j):
            closest = group * (t - key_slot) - (group - 1)
            farthest = group * (t - key_slot) + (group - 1)
            s = contract(kv[0, j], query, 1, 1) * scale
            grad_probs = contract(kv[1, j], grad, 1, 1)
            ahead = (slab - j) * rows
            higher = jnp.int32(0)
            for l in range(1, level_count):
                higher += jnp.where((slab >> l) != (j >> l), 1, 0)
            distance = (
                lax.broadcasted_iota(jnp.int32, (rows, rows), 1)
                - lax.broadcasted_iota(jnp.int32, (rows, rows), 0)
                + ahead
            )
            count = jnp.maximum(level[...] - higher.astype(jnp.float32), 0.0)
            inside = (farthest + 1) * rows - 1 < WINDOW
            if inside:
                count += 1.0
            elif (closest - 1) * rows + 1 < WINDOW:
                count += jnp.where(distance < WINDOW, 1.0, 0.0)
            if closest < 1:
                count = jnp.where(distance >= 0, count, 0.0)
            if not inside or closest < 1:
                s = jnp.where(count > 0.0, s, MASKED)
            probs[j] = grad_probs
            return s, count, grad_probs

        def score(key_slot, i, carry):
            row_max, row_sum, row_dot = carry
            first = key_slot * group + i * step_blocks
            parts = [masked(key_slot, first + n) for n in range(step_blocks)]
            highest = functools.reduce(jnp.maximum, [part[0] for part in parts])
            top = jnp.maximum(row_max, jnp.max(highest, axis=0, keepdims=True))
            fade = jnp.exp(row_max - top)
            weights, dots = 0.0, 0.0
            for n, (s, count, grad_probs) in enumerate(parts):
                e = count * jnp.exp(s - top)
                scores[first + n] = e
                tops[first + n] = top
                weights += e
                dots += e * grad_probs
            row_sum = row_sum * fade + jnp.sum(weights, axis=0, keepdims=True)
            row_dot = row_dot * fade + jnp.sum(dots, axis=0, keepdims=True)
            return top, row_sum, row_dot

        zero = jnp.zeros((1, rows), jnp.float32)
        start = (jnp.full((1, rows), MASKED, jnp.float32), zero, zero)
        for key_slot in range(t + 1):
            start = lax.fori_loop(
                0, group // step_blocks, functools.partial(score, key_slot), start
            )
        row_max, row_sum, row_dot = start
        inverse = 1.0 / row_sum
        grad_dot = row_dot * inverse

        def differentiate(j, dq):
            p = scores[j] * (jnp.exp(tops[j] - row_max) * inverse)
            ds = (p * (probs[j] - grad_dot)).astype(jnp.bfloat16)
            total[1, j] += contract(p.astype(jnp.bfloat16), grad, 1, 0)
            total[0, j] += contract(ds, query, 1, 0)
            return dq + contract(kv[0, j], ds, 0, 0)

        dq = jnp.zeros((width, rows), jnp.float32)
        if t < slots - 1:
            share_out(t + 1)
            for key_slot in range(t + 1):
                dq = lax.fori_loop(
                    key_slot * group, (key_slot + 1) * group, differentiate, dq, unroll=2
                )
        else:
            for step in range(slots):
                j = far_first(step, slots)
                dq = lax.fori_loop(
                    0, group, lambda i, dq: differentiate(j * group + i, dq), dq, unroll=2
                )
                swap(j)
                if step > 0:
                    settle(far_first(step - 1, slots))
        dq_out[t] = (dq * scale).T.astype(jnp.bfloat16)
        move(*outward(0, t))

    factors = (scale, 1.0)

    def partial_sum(a, t, r):
        return remote(
            part_out.at[r - 1, a, t],
            part_in.at[r - 1, a, t],
            part_send.at[r - 1, a, t],
            part_recv.at[r - 1, a, t],
            peer(r)[1],
        )

    def swap(t):
        for r in range(1, group):
            for a in range(2):
                value = total[a, peer(r)[0] + group * t] * factors[a]
                part_out[r - 1, a, t] = value.astype(jnp.bfloat16)
                partial_sum(a, t, r).start()

    def settle(t):
        for a in range(2):
            value = total[a, share + group * t] * factors[a]
            for r in range(1, group):
                partial_sum(a, t, r).wait_recv()
                value += part_in[r - 1, a, t].astype(jnp.float32)
            kv_out[a, t] = value.astype(jnp.bfloat16)
            move(*outward(a + 1, t))

    share_out(0)
    for t in range(slots):
        work(t)
    settle(far_first(slots - 1, slots))

    for a, ref in enumerate((dq_ref, dk_ref, dv_ref)):
        for h in range(heads):
            landed(ref.at[:, pl.ds(h * width, width)], out_recv.at[a, h])
        for t in range(slots):
            sent(*outward(a, t))
    for a in range(4):
        for h in range(heads):
            sent(*inward(a, h))
    for a in range(2):
        for t in range(slots):
            for r in range(1, group):
                shared(a, t, r).wait_send()
                partial_sum(a, t, r).wait_send()


def hand_over(*refs):
    for source, target in zip(refs[:3], refs[3:]):
        target[...] = source[...]


def body(devices, batches, query_states, key_states, value_states, out_grad, head_offsets):
    rows, heads = query_states.shape[0], head_offsets.shape[0]
    width = query_states.shape[1] // heads
    group = devices // heads
    slots = devices // group
    half, full = jnp.bfloat16, jnp.float32
    anywhere = pl.BlockSpec(memory_space=pl.ANY)
    dma = pltpu.SemaphoreType.DMA
    result = jax.ShapeDtypeStruct(query_states.shape, half)
    landed = pl.pallas_call(
        functools.partial(kernel, devices, batches, heads),
        out_shape=(result,) * 3,
        in_specs=[pl.BlockSpec(memory_space=pltpu.SMEM)] + [anywhere] * 4,
        out_specs=(anywhere,) * 3,
        scratch_shapes=[
            pltpu.VMEM((2, devices, rows, width), half),
            pltpu.VMEM((2, slots, rows, width), half),
            pltpu.VMEM((devices, rows, rows), full),
            pltpu.VMEM((devices, rows, rows), full),
            pltpu.VMEM((devices, 1, rows), full),
            pltpu.VMEM((rows, rows), full),
            pltpu.VMEM((2, devices, rows, width), full),
            pltpu.VMEM((slots, rows, width), half),
            pltpu.VMEM((group - 1, 2, slots, rows, width), half),
            pltpu.VMEM((group - 1, 2, slots, rows, width), half),
            pltpu.VMEM((2, slots, rows, width), half),
            dma((4, heads)),
            dma((2, devices)),
            dma((2, slots)),
            dma((group - 1, 2, slots)),
            dma((group - 1, 2, slots)),
            dma((group - 1, 2, slots)),
            dma((3, slots)),
            dma((3, heads)),
        ],
        compiler_params=pltpu.CompilerParams(
            collective_id=0, has_side_effects=True, vmem_limit_bytes=56 * 2**20
        ),
    )(head_offsets, key_states, value_states, query_states, out_grad)
    return pl.pallas_call(hand_over, out_shape=(result,) * 3)(*landed)


def solution(mesh):
    slab = P(("batch", "seq"), "head")
    return jax.shard_map(
        functools.partial(body, mesh.shape["seq"], mesh.shape["batch"]),
        mesh=mesh,
        in_specs=(slab,) * 4 + (P("head"),),
        out_specs=(slab,) * 3,
        check_vma=False,
    )
```
